32 devices in a mesh: groups: 2 (over y), row: 4 (over x, core), col: 4 (over z).
Axes of the slice: x: 2, y: 2, z: 4, core: 2. Of those that a mesh axis runs over, the one named last changes fastest.
Arguments:
- pair: bfloat16 [1280, 640, 128], P(('groups', 'row'), 'col'), parts along dimension 0, may hold values from -6 to 6
- product: bfloat16 [1280, 640, 128], P(('groups', 'row'), 'col'), parts along dimension 0, may hold values from -6 to 6
- mask: int32 [1280, 640], P(('groups', 'row'), 'col'), parts along dimension 0, may hold values 0 or 1
- grad_out: bfloat16 [1280, 640, 128], P(('groups', 'row'), 'col'), parts along dimension 0, may hold values from -6 to 6
- weights: bfloat16 [6, 128, 128], replicated, may hold values from -0.5 to 0.5
- norms: float32 [4, 128], replicated, may hold values from 0.25 to 1.75
Outputs:
- grad_pair: bfloat16 [1280, 640, 128], P(('groups', 'row'), 'col'), parts along dimension 0
- grad_weights: float32 [12, 128, 128], P('groups'), parts along dimension 0
- norm_vector_gradients: float32 [8, 128], P('groups'), parts along dimension 0
The draws below stay inside these ranges and needn't reach their ends.
There are 2 independent parts, one for each index of `groups`. The reference program is written for one: setup_inputs(seed, part) draws one part's arguments, and reference() takes and returns one part's arrays. A program takes and returns all parts, laid end to end along the dimension named above; an argument that names none is the same for every part. Nothing has to cross between parts.
Inputs may be any that keep to these rules, and one draw needn't show every extreme that they name: `mask`: 0 marks an invalid pair, 1 a valid one.
All inputs are finite; a program needn't handle non-finite values. No bound on the sum of `mask` on one device may be relied on, other than what follows from the above.
Results may differ from the reference program's by a relative error of at most 0.01.
Values may be sent and summed in bfloat16 or wider, within the bound.
No kernel may reach another device: no remote copies, remote signals or barrier semaphores. Data moves between devices by JAX's collectives and lax.ppermute only.
A program may use at most 448 MiB of HBM per device.

```python
import jax
import jax.numpy as jnp
from jax import lax

C = 128
N = 640
N_ROW = 4


def set_ends(drawn, rng, smallest, high):
    longest = drawn.shape.index(max(drawn.shape))
    spots = []
    for shift in (0, 1):
        where = [jax.random.randint(jax.random.fold_in(rng, axis), (), 0, length) for axis, length in enumerate(drawn.shape)]
        where[longest] = (where[longest] + shift) % drawn.shape[longest]
        spots.append(tuple(where))
    return drawn.at[spots[0]].set(smallest).at[spots[1]].set(high)


def block_levels(own_key, dims, shards, smallest, high):
    factor_of, own = 1.0, jax.random.fold_in(own_key, 6)
    for axis_at, blocks in shards:
        draws = jnp.exp(jax.random.uniform(jax.random.fold_in(own, axis_at), (blocks,), jnp.float32, smallest / len(shards), high / len(shards)))
        factor_of = factor_of * jnp.repeat(draws, dims[axis_at] // blocks).reshape([-1 if axis == axis_at else 1 for axis in range(len(dims))])
    return factor_of


def centred(key, extent, deviation, reach, split=(), held_as=jnp.bfloat16):
    drawn = jax.random.normal(key, extent, jnp.float32) * deviation
    if len(split) > 0:
        drawn = block_levels(key, extent, split, -0.22, 0.18) * drawn
    return jnp.clip(drawn, min=-reach, max=reach).astype(held_as)


def setup_inputs(seed: int = 0, part: int = 0) -> dict:
    key_list = jax.random.split(jax.random.key(seed), 7)
    part_splits = jax.random.split(jax.random.fold_in(key_list[6], part), 7)
    return {
        "pair": centred(part_splits[0], (N, N, C), 1.0, 6.0, ((0, 4), (1, 4))),
        "product": centred(part_splits[1], (N, N, C), 1.0, 6.0, ((0, 4), (1, 4))),
        "mask": set_ends((jax.random.randint(part_splits[2], (N, N), 0, 8) < 7).astype(jnp.int32), jax.random.fold_in(part_splits[2], 1), 0, 1),
        "grad_out": centred(part_splits[3], (N, N, C), 1.0, 6.0, ((0, 4), (1, 4))),
        "weights": centred(key_list[4], (6, C, C), C ** -0.5, 0.5),
        "norms": jnp.clip(1.0 + 0.15 * jax.random.normal(key_list[5], (4, C), jnp.float32), 0.25, 1.75),
    }


eps = 1e-05

def layer_normalize(v):
    mean = lax.optimization_barrier(jnp.mean(v, axis=-1, keepdims=True))
    cent = v - mean
    inv = lax.rsqrt(lax.optimization_barrier(jnp.mean(cent * cent, axis=-1, keepdims=True)) + eps)
    return (cent * inv, inv)

def layer_norm_backward(grad, centered_scaled, inv):
    return inv * (grad - lax.optimization_barrier(jnp.mean(grad, axis=-1, keepdims=True)) - centered_scaled * lax.optimization_barrier(jnp.mean(grad * centered_scaled, axis=-1, keepdims=True)))

def reference(pair, product, mask, grad_out, weights, norms):
    channel_total = pair.shape[-1]
    element_count = pair.shape[0] * pair.shape[1]
    centered_scaled, inv = layer_normalize(pair.astype(jnp.float32).reshape(element_count, channel_total))
    zn = (centered_scaled * norms[0] + norms[1]).astype(jnp.bfloat16)
    wcat = jnp.transpose(weights[:5], (1, 0, 2)).reshape(channel_total, 5 * channel_total)
    logits = jnp.dot(zn, wcat, preferred_element_type=jnp.float32)
    ga = jax.nn.sigmoid(logits[:, 0:channel_total])
    pa = logits[:, channel_total:2 * channel_total]
    gb = jax.nn.sigmoid(logits[:, 2 * channel_total:3 * channel_total])
    pb = logits[:, 3 * channel_total:4 * channel_total]
    og = jax.nn.sigmoid(logits[:, 4 * channel_total:])
    valid = mask.astype(jnp.float32).reshape(element_count, 1)
    a_proj = (valid * ga * pa).astype(jnp.bfloat16)
    b_proj = (valid * gb * pb).astype(jnp.bfloat16)
    standardized_input, inverse_deviation_squared = layer_normalize(product.astype(jnp.float32).reshape(element_count, channel_total))
    normed_input = (standardized_input * norms[2] + norms[3]).astype(jnp.bfloat16)
    y_out = jnp.dot(normed_input, weights[5], preferred_element_type=jnp.float32)
    go = grad_out.astype(jnp.float32).reshape(element_count, channel_total)
    d_og = go * y_out
    d_y = (go * og).astype(jnp.bfloat16)
    normed_input_gradient = jnp.dot(d_y, weights[5].T, preferred_element_type=jnp.float32)
    input_gradient = layer_norm_backward(normed_input_gradient * norms[2], standardized_input, inverse_deviation_squared).astype(jnp.bfloat16)
    d_ologit = (d_og * og * (1.0 - og)).astype(jnp.bfloat16)
    side = pair.shape[0]
    dx3 = input_gradient.reshape(side, side, channel_total).astype(jnp.float32)
    a3 = a_proj.reshape(side, side, channel_total).astype(jnp.float32)
    b3 = b_proj.reshape(side, side, channel_total).astype(jnp.float32)
    da = jnp.einsum('ijc,jkc->ikc', dx3, b3).reshape(element_count, channel_total)
    block = side // N_ROW
    dx_blocks = dx3.reshape(N_ROW, block, side, channel_total)
    a_blocks = a3.reshape(N_ROW, block, side, channel_total)

    def add_block(total, pieces):
        part = jnp.einsum('ijc,ikc->jkc', pieces[0], pieces[1])
        return (total + part.astype(jnp.bfloat16).astype(jnp.float32), None)
    db, _ = lax.scan(add_block, jnp.zeros((side, side, channel_total), jnp.float32), (dx_blocks, a_blocks))
    db = db.reshape(element_count, channel_total)
    d_pa = da * valid * ga
    d_ga = da * valid * pa * ga * (1.0 - ga)
    d_pb = db * valid * gb
    d_gb = db * valid * pb * gb * (1.0 - gb)
    dcat = jnp.concatenate([d_ga, d_pa, d_gb, d_pb], axis=1).astype(jnp.bfloat16)
    dcat = jnp.concatenate([dcat, d_ologit], axis=1)
    normed_output_gradient = jnp.dot(dcat, wcat.T, preferred_element_type=jnp.float32)
    grad_pair = layer_norm_backward(normed_output_gradient * norms[0], centered_scaled, inv).astype(jnp.bfloat16).reshape(side, side, channel_total)
    gw = jnp.dot(zn.T, dcat, preferred_element_type=jnp.float32)
    gw = jnp.transpose(gw.reshape(channel_total, 5, channel_total), (1, 0, 2))
    gwo = jnp.dot(normed_input.T, d_y, preferred_element_type=jnp.float32)
    grad_weights = jnp.concatenate([gw, gwo[None]], axis=0)
    norm_vector_gradients = jnp.stack([lax.optimization_barrier(jnp.sum(normed_output_gradient * centered_scaled, axis=0)), lax.optimization_barrier(jnp.sum(normed_output_gradient, axis=0)), lax.optimization_barrier(jnp.sum(normed_input_gradient * standardized_input, axis=0)), lax.optimization_barrier(jnp.sum(normed_input_gradient, axis=0))])
    return (grad_pair, grad_weights, norm_vector_gradients)
```

```python
import functools

import jax
import jax.numpy as jnp
from jax import lax
from jax.experimental import pallas as pl
from jax.experimental.pallas import tpu as pltpu
from jax.sharding import PartitionSpec as P

eps = 1e-05
F32 = jnp.float32
BF16 = jnp.bfloat16
VMEM_LIMIT = 48 * 1024 * 1024


def dot(x, y):
    return jnp.dot(x, y, preferred_element_type=F32)


def dot_t(x, y):
    return lax.dot_general(x, y, (((1,), (1,)), ((), ())), preferred_element_type=F32)


def t_dot(x, y):
    return lax.dot_general(x, y, (((0,), (0,)), ((), ())), preferred_element_type=F32)


def layer_normalize(v):
    mean = jnp.mean(v, axis=-1, keepdims=True)
    cent = v - mean
    inv = lax.rsqrt(jnp.mean(cent * cent, axis=-1, keepdims=True) + eps)
    return cent * inv, inv


def layer_norm_backward(grad, hat, inv):
    return inv * (
        grad
        - jnp.mean(grad, axis=-1, keepdims=True)
        - hat * jnp.mean(grad * hat, axis=-1, keepdims=True)
    )


def tile(ref, s, step):
    block = ref[pl.ds(s * step, step)]
    return block.reshape(-1, block.shape[-1])


def put(ref, s, step, value):
    ref[pl.ds(s * step, step)] = value.reshape((step,) + ref.shape[1:]).astype(ref.dtype)


def first_step(axes):
    first = pl.program_id(0) == 0
    for axis in range(1, axes):
        first = jnp.logical_and(first, pl.program_id(axis) == 0)
    return first


def dx_kernel(step, chained, pair, product, go, w, norms, *rest):
    acc_in = rest[1] if chained else None
    dx, dol, acc = rest[-3:]
    c = pair.shape[-1]

    @pl.when(first_step(2))
    def _():
        acc[...] = acc_in[...] if chained else jnp.zeros_like(acc)

    def body(s, carry):
        hat, _ = layer_normalize(tile(pair, s, step).astype(F32))
        zn = (hat * norms[0:1] + norms[1:2]).astype(BF16)
        og = jax.nn.sigmoid(dot(zn, w[4]))
        xhat, inv2 = layer_normalize(tile(product, s, step).astype(F32))
        xn = (xhat * norms[2:3] + norms[3:4]).astype(BF16)
        y = dot(xn, w[5])
        gof = tile(go, s, step).astype(F32)
        d_y = (gof * og).astype(BF16)
        d_xn = dot_t(d_y, w[5])
        put(dx, s, step, layer_norm_backward(d_xn * norms[2:3], xhat, inv2))
        put(dol, s, step, gof * y * og * (1.0 - og))
        acc[5 * c : 6 * c] += t_dot(xn, d_y)
        acc[6 * c + 2 : 6 * c + 3] += jnp.sum(d_xn * xhat, axis=0, keepdims=True)
        acc[6 * c + 3 : 6 * c + 4] += jnp.sum(d_xn, axis=0, keepdims=True)
        return carry

    lax.fori_loop(0, pair.shape[0] // step, body, 0)


def dx_chunk(pair, product, go, weights, norms, off, size, chain):
    rows, cols, c = pair.shape
    jb = 16 if size % 16 == 0 else size
    ib = 80 if rows % 80 == 0 else rows // 2 if rows % 2 == 0 else rows
    step = 16 if ib % 16 == 0 else ib
    base = off // jb
    blk = pl.BlockSpec((ib, jb, c), lambda i, j: (i, base + j, 0))
    out = pl.BlockSpec((ib, jb, c), lambda i, j: (i, j, 0))
    full = lambda shape: pl.BlockSpec(shape, lambda i, j: (0,) * len(shape))
    n = rows * size
    acc = (6 * c + 32, c)
    return pl.pallas_call(
        functools.partial(dx_kernel, step, bool(chain)),
        grid=(rows // ib, size // jb),
        in_specs=[blk, blk, blk, full(weights.shape), full(norms.shape)]
        + ([pl.BlockSpec(memory_space=pl.ANY), full(acc)] if chain else []),
        out_specs=[out, blk, full(acc)],
        out_shape=[
            jax.ShapeDtypeStruct((rows, size, c), BF16),
            jax.ShapeDtypeStruct((rows, cols, c), BF16),
            jax.ShapeDtypeStruct(acc, F32),
        ],
        input_output_aliases={5: 1} if chain else {},
        compiler_params=pltpu.CompilerParams(vmem_limit_bytes=VMEM_LIMIT),
        cost_estimate=pl.CostEstimate(
            flops=8 * n * c * c, bytes_accessed=10 * n * c, transcendentals=n * c
        ),
        name="dx_part",
    )(pair, product, go, weights, norms, *chain)


def proj_kernel(step, pair, valid, w, norms, a, b, g_ga, g_pa, g_gb, g_pb, flip):
    cols, c = pair.shape[1:]

    def body(s, carry):
        hat, _ = layer_normalize(tile(pair, s, step).astype(F32))
        zn = (hat * norms[0:1] + norms[1:2]).astype(BF16)
        m = tile(valid, s, step).astype(F32)
        for at, d_gate, d_value in ((0, g_ga, g_pa), (2, g_gb, g_pb)):
            gate = jax.nn.sigmoid(dot(zn, w[at]))
            p = dot(zn, w[at + 1])
            mg = m * gate
            mgp = mg * p
            if at == 0:
                put(a, s, step, mgp)
            else:
                flip[pl.ds(s * step, step)] = mgp.reshape(step, cols, c)
            put(d_value, s, step, mg)
            put(d_gate, s, step, mgp * (1.0 - gate))
        return carry

    lax.fori_loop(0, pair.shape[0] // step, body, 0)
    b[...] = jnp.swapaxes(flip[...], 0, 1).astype(b.dtype)


def projections(pair, valid, weights, norms):
    rows, cols, c = pair.shape
    ib = 16 if rows % 16 == 0 else rows
    step = 2
    blk = pl.BlockSpec((ib, cols, c), lambda i: (i, 0, 0))
    swapped = pl.BlockSpec((cols, ib, c), lambda i: (0, i, 0))
    full = lambda shape: pl.BlockSpec(shape, lambda i: (0,) * len(shape))
    n = rows * cols
    kept = jax.ShapeDtypeStruct((rows, cols, c), BF16)
    return pl.pallas_call(
        functools.partial(proj_kernel, step),
        grid=(rows // ib,),
        in_specs=[blk, blk, full(weights.shape), full(norms.shape)],
        out_specs=[blk, swapped] + [blk] * 4,
        out_shape=[kept, jax.ShapeDtypeStruct((cols, rows, c), BF16)] + [kept] * 4,
        scratch_shapes=[pltpu.VMEM((ib, cols, c), F32)],
        compiler_params=pltpu.CompilerParams(vmem_limit_bytes=VMEM_LIMIT),
        cost_estimate=pl.CostEstimate(
            flops=8 * n * c * c, bytes_accessed=16 * n * c, transcendentals=2 * n * c
        ),
        name="projections",
    )(pair, valid, weights, norms)


def to_channels_kernel(slots, r, *refs):
    out = refs[-1]
    blocks = [ref[...].reshape(ref.shape[-3:]) for ref in refs[:-1]]
    x = jnp.concatenate(blocks, axis=1)
    out[...] = jnp.transpose(x, (2, 0, 1))


def to_channels(arrays, specs, r, lead, size, c):
    slots = len(specs)
    lanes = slots * size
    n = lead * lanes * c
    return pl.pallas_call(
        functools.partial(to_channels_kernel, slots),
        grid_spec=pltpu.PrefetchScalarGridSpec(
            num_scalar_prefetch=1,
            grid=(lead // 16,),
            in_specs=specs,
            out_specs=pl.BlockSpec((c, 16, lanes), lambda i, r: (0, i, 0)),
        ),
        out_shape=jax.ShapeDtypeStruct((c, lead, lanes), BF16),
        compiler_params=pltpu.CompilerParams(vmem_limit_bytes=VMEM_LIMIT),
        cost_estimate=pl.CostEstimate(flops=4 * n, bytes_accessed=4 * n, transcendentals=0),
        name="to_channels",
    )(r, *arrays)


def gathered_to_channels(g, r):
    n, rows, size, c = g.shape
    specs = [
        pl.BlockSpec((1, 16, size, c), lambda i, r, t=t: (r[0] ^ t, i, 0, 0)) for t in range(n)
    ]
    return to_channels([g] * n, specs, r, rows, size, c)


def slots_to_channels(slots, r, off, size):
    lead, _, c = slots[0].shape
    specs = [pl.BlockSpec((16, size, c), lambda i, r: (i, off // size, 0))] * len(slots)
    return to_channels(slots, specs, r, lead, size, c)


def from_channels_kernel(slots, x, kept, sent):
    y = jnp.transpose(x[...], (1, 2, 0))
    size = y.shape[1] // slots
    for t in range(slots):
        out = sent if t % 2 else kept
        out[t // 2] = y[:, t * size : (t + 1) * size]


def from_channels(x, slots):
    c, lead, lanes = x.shape
    size = lanes // slots
    n = x.size
    out = pl.BlockSpec((slots // 2, 16, size, c), lambda i: (0, i, 0, 0))
    return pl.pallas_call(
        functools.partial(from_channels_kernel, slots),
        grid=(lead // 16,),
        in_specs=[pl.BlockSpec((c, 16, lanes), lambda i: (0, i, 0))],
        out_specs=[out, out],
        out_shape=[jax.ShapeDtypeStruct((slots // 2, lead, size, c), BF16)] * 2,
        compiler_params=pltpu.CompilerParams(vmem_limit_bytes=VMEM_LIMIT),
        cost_estimate=pl.CostEstimate(flops=4 * n, bytes_accessed=4 * n, transcendentals=0),
        name="from_channels",
    )(x)


def final_kernel(step, chained, pair, da, db0, db1, g_ga, g_pa, g_gb, g_pb, dol, w, norms, acc_in, *rest):
    gp, acc, flip = rest[-3:]
    c = pair.shape[-1]

    @pl.when(first_step(1))
    def _():
        acc[...] = acc_in[...]

    flip[...] = jnp.swapaxes(db0[...].astype(F32) + db1[...].astype(F32), 0, 1)

    def body(s, carry):
        hat, inv = layer_normalize(tile(pair, s, step).astype(F32))
        zn = (hat * norms[0:1] + norms[1:2]).astype(BF16)
        dav = tile(da, s, step).astype(F32)
        dbv = tile(flip, s, step)
        parts = [
            (dav * tile(g_ga, s, step).astype(F32)).astype(BF16),
            (dav * tile(g_pa, s, step).astype(F32)).astype(BF16),
            (dbv * tile(g_gb, s, step).astype(F32)).astype(BF16),
            (dbv * tile(g_pb, s, step).astype(F32)).astype(BF16),
            tile(dol, s, step),
        ]
        dzn = dot_t(parts[0], w[0])
        for at in range(1, 5):
            dzn = dzn + dot_t(parts[at], w[at])
        put(gp, s, step, layer_norm_backward(dzn * norms[0:1], hat, inv))
        for at in range(5):
            acc[at * c : (at + 1) * c] += t_dot(zn, parts[at])
        acc[6 * c : 6 * c + 1] += jnp.sum(dzn * hat, axis=0, keepdims=True)
        acc[6 * c + 1 : 6 * c + 2] += jnp.sum(dzn, axis=0, keepdims=True)
        return carry

    lax.fori_loop(0, pair.shape[0] // step, body, 0)


def final_chunk(pair, da, db0, db1, gs, dol, weights, norms, acc, off, size, chain):
    rows, cols, c = pair.shape
    ib = 16 if size % 16 == 0 else size
    step = 2
    base = off // ib
    blk = pl.BlockSpec((ib, cols, c), lambda i: (base + i, 0, 0))
    own = pl.BlockSpec((cols, ib, c), lambda i: (0, i, 0))
    full = lambda shape: pl.BlockSpec(shape, lambda i: (0,) * len(shape))
    n = size * cols
    return pl.pallas_call(
        functools.partial(final_kernel, step, bool(chain)),
        grid=(size // ib,),
        in_specs=[blk, blk, own, own]
        + [blk] * 5
        + [full(weights.shape), full(norms.shape), full(acc.shape)]
        + ([pl.BlockSpec(memory_space=pl.ANY)] if chain else []),
        out_specs=[blk, full(acc.shape)],
        out_shape=[
            jax.ShapeDtypeStruct((rows, cols, c), BF16),
            jax.ShapeDtypeStruct(acc.shape, F32),
        ],
        input_output_aliases={12: 0} if chain else {},
        scratch_shapes=[pltpu.VMEM((ib, cols, c), F32)],
        compiler_params=pltpu.CompilerParams(vmem_limit_bytes=VMEM_LIMIT),
        cost_estimate=pl.CostEstimate(
            flops=20 * n * c * c, bytes_accessed=22 * n * c, transcendentals=n
        ),
        name="final_part",
    )(pair, da, db0, db1, *gs, dol, weights, norms, acc, *chain)


def swap(v, axis, n, bit):
    return lax.ppermute(v, axis, [(r, r ^ bit) for r in range(n)])


def pick(v, at):
    return lax.dynamic_index_in_dim(v, at, 0, keepdims=False)


def bits_of(n):
    return [1 << k for k in range(n.bit_length() - 1)]


def gather_rows(v, n):
    slots = {0: v}
    for bit in bits_of(n)[::-1]:
        slots.update({t ^ bit: swap(x, "row", n, bit) for t, x in slots.items()})
    return [slots[t] for t in range(n)]


def reduce_rows(kept, sent, n):
    come = swap(sent, "row", n, 1)
    for bit in bits_of(n)[1:]:
        v = (kept.astype(F32) + come.astype(F32)).astype(BF16)
        v = v.reshape((-1, 2) + v.shape[1:])
        kept, come = v[:, 0], swap(v[:, 1], "row", n, bit)
    return kept[0], come[0]


def sum_all(v, n_row, n_col):
    steps = [("row", n_row, b) for b in bits_of(n_row)] + [("col", n_col, b) for b in bits_of(n_col)]
    halved = []
    for k, (axis, n, bit) in enumerate(steps):
        half = v.shape[0] // 2
        if 0 < k < len(steps) - 1 and v.shape[0] % 16 == 0:
            at = (lax.axis_index(axis) // bit) % 2
            pairs = v.reshape((2, half) + v.shape[1:])
            v = pick(pairs, at) + swap(pick(pairs, 1 - at), axis, n, bit)
            halved.append((axis, n, bit, at))
        else:
            v = v + swap(v, axis, n, bit)
    for axis, n, bit, at in halved[::-1]:
        got = swap(v, axis, n, bit)
        v = jnp.where(at == 0, jnp.concatenate([v, got]), jnp.concatenate([got, v]))
    return v


def triangles_plain(n_row, n_col, dx, a, b_swapped):
    rows, cols, c = dx.shape
    block = lax.all_gather(dx, "col", axis=1, tiled=True)
    b_all = lax.all_gather(b_swapped, "row", axis=1, tiled=True)
    part = jnp.einsum("ijc,ikc->kjc", block, a, preferred_element_type=F32).astype(BF16)
    db = lax.psum_scatter(part, "row", scatter_dimension=1, tiled=True)
    da = jnp.einsum("ijc,kjc->ikc", block, b_all, preferred_element_type=F32)
    return da.astype(BF16), [(db, jnp.zeros_like(db))], [(0, rows)]


def triangles(n, blocks, spans, a, b_swapped):
    r = lax.axis_index("row").astype(jnp.int32).reshape(1)
    b_slots = gather_rows(b_swapped, n)
    a_t = jnp.transpose(a, (2, 0, 1))
    da = None
    db = []
    for block, (off, size) in zip(blocks, spans):
        if da is not None:
            block, da = lax.optimization_barrier((block, da))
        dx_t = gathered_to_channels(block, r)
        part = jnp.einsum("cik,cij->ckj", a_t, dx_t, preferred_element_type=F32).astype(BF16)
        kept, sent = from_channels(part, n)
        db.append(reduce_rows(kept, sent, n))
        dx_t, sent = lax.optimization_barrier((dx_t, sent))
        b_t = slots_to_channels(b_slots, r, off, size)
        term = jnp.einsum("cij,ckj->cik", dx_t, b_t, preferred_element_type=F32)
        da = term if da is None else da + term
    return jnp.transpose(da.astype(BF16), (1, 2, 0)), db, spans


def shards(n_row, n_col, pair, product, mask, grad_out, weights, norms):
    rows, cols, c = pair.shape
    even = n_row == n_col and n_row & (n_row - 1) == 0 and cols % 32 == 0 and rows % 16 == 0
    size = 32 if even else cols
    spans = [(off, size) for off in range(0, cols, size)]
    pieces, chain = [], []
    for off, size in spans:
        dx, *chain = dx_chunk(pair, product, grad_out, weights, norms, off, size, chain)
        pieces.append(lax.all_gather(dx, "col", axis=0) if even else dx)
    dol, acc = chain
    valid = jnp.broadcast_to(mask.astype(BF16)[:, :, None], pair.shape)
    a, b_swapped, *gs = projections(pair, valid, weights, norms)
    if even:
        da, db, spans = triangles(n_row, pieces, spans, a, b_swapped)
    else:
        da, db, spans = triangles_plain(n_row, n_col, pieces[0], a, b_swapped)
    chain = []
    for (db0, db1), (off, size) in zip(db, spans):
        grad_pair, acc = final_chunk(
            pair, da, db0, db1, gs, dol, weights, norms, acc, off, size, chain
        )
        chain = [grad_pair]
    acc = sum_all(acc, n_row, n_col)
    return (grad_pair, acc[: 6 * c].reshape(6, c, c), acc[6 * c : 6 * c + 4])


def solution(mesh):
    in_specs = (
        P(("groups", "row"), "col", None),
        P(("groups", "row"), "col", None),
        P(("groups", "row"), "col"),
        P(("groups", "row"), "col", None),
        P(),
        P(),
    )
    out_specs = (P(("groups", "row"), "col", None), P("groups", None, None), P("groups", None))
    body = functools.partial(shards, mesh.shape["row"], mesh.shape["col"])
    return jax.shard_map(body, mesh=mesh, in_specs=in_specs, out_specs=out_specs, check_vma=False)
```

```python
import functools

import jax
import jax.numpy as jnp
from jax import lax
from jax.experimental import pallas as pl
from jax.experimental.layout import Layout, with_layout_constraint
from jax.experimental.pallas import tpu as pltpu
from jax.sharding import PartitionSpec as P

eps = 1e-05
F32 = jnp.float32
BF16 = jnp.bfloat16
VMEM_LIMIT = 48 * 1024 * 1024


def dot(x, y):
    return jnp.dot(x, y, preferred_element_type=F32)


def sigmoid(x):
    return 0.5 * jnp.tanh(0.5 * x) + 0.5


def dot_t(x, y):
    return lax.dot_general(x, y, (((1,), (1,)), ((), ())), preferred_element_type=F32)


def t_dot(x, y):
    return lax.dot_general(x, y, (((0,), (0,)), ((), ())), preferred_element_type=F32)


def layer_normalize(v):
    mean = jnp.mean(v, axis=-1, keepdims=True)
    cent = v - mean
    inv = lax.rsqrt(jnp.mean(cent * cent, axis=-1, keepdims=True) + eps)
    return cent * inv, inv


def layer_norm_backward(grad, hat, inv):
    return inv * (
        grad
        - jnp.mean(grad, axis=-1, keepdims=True)
        - hat * jnp.mean(grad * hat, axis=-1, keepdims=True)
    )


def tile(ref, s, step):
    block = ref[pl.ds(s * step, step)]
    return block.reshape(-1, block.shape[-1])


def put(ref, s, step, value):
    ref[pl.ds(s * step, step)] = value.reshape((step,) + ref.shape[1:]).astype(ref.dtype)


def first_step(axes):
    first = pl.program_id(0) == 0
    for axis in range(1, axes):
        first = jnp.logical_and(first, pl.program_id(axis) == 0)
    return first


def dx_kernel(step, chained, pair, product, go, w, norms, *rest):
    acc_in = rest[1] if chained else None
    dx, dol, acc = rest[-3:]
    c = pair.shape[-1]

    @pl.when(first_step(2))
    def _():
        acc[...] = acc_in[...] if chained else jnp.zeros_like(acc)

    def body(s, carry):
        hat, _ = layer_normalize(tile(pair, s, step).astype(F32))
        zn = (hat * norms[0:1] + norms[1:2]).astype(BF16)
        og = sigmoid(dot(zn, w[4]))
        xhat, inv2 = layer_normalize(tile(product, s, step).astype(F32))
        xn = (xhat * norms[2:3] + norms[3:4]).astype(BF16)
        y = dot(xn, w[5])
        gof = tile(go, s, step).astype(F32)
        d_y = (gof * og).astype(BF16)
        d_xn = dot_t(d_y, w[5])
        put(dx, s, step, layer_norm_backward(d_xn * norms[2:3], xhat, inv2))
        put(dol, s, step, gof * y * og * (1.0 - og))
        acc[5 * c : 6 * c] += t_dot(xn, d_y)
        acc[6 * c + 2 : 6 * c + 3] += jnp.sum(d_xn * xhat, axis=0, keepdims=True)
        acc[6 * c + 3 : 6 * c + 4] += jnp.sum(d_xn, axis=0, keepdims=True)
        return carry

    lax.fori_loop(0, pair.shape[0] // step, body, 0)


def dx_chunk(pair, product, go, weights, norms, off, size, chain):
    rows, cols, c = pair.shape
    jb = 16 if size % 16 == 0 else size
    ib = 80 if rows % 80 == 0 else rows // 2 if rows % 2 == 0 else rows
    step = 40 if ib % 40 == 0 else ib
    base = off // jb
    blk = pl.BlockSpec((ib, jb, c), lambda i, j: (i, base + j, 0))
    out = pl.BlockSpec((ib, jb, c), lambda i, j: (i, j, 0))
    full = lambda shape: pl.BlockSpec(shape, lambda i, j: (0,) * len(shape))
    n = rows * size
    acc = (6 * c + 32, c)
    return pl.pallas_call(
        functools.partial(dx_kernel, step, bool(chain)),
        grid=(rows // ib, size // jb),
        in_specs=[blk, blk, blk, full(weights.shape), full(norms.shape)]
        + ([pl.BlockSpec(memory_space=pl.ANY), full(acc)] if chain else []),
        out_specs=[out, blk, full(acc)],
        out_shape=[
            jax.ShapeDtypeStruct((rows, size, c), BF16),
            jax.ShapeDtypeStruct((rows, cols, c), BF16),
            jax.ShapeDtypeStruct(acc, F32),
        ],
        input_output_aliases={5: 1} if chain else {},
        compiler_params=pltpu.CompilerParams(vmem_limit_bytes=VMEM_LIMIT),
        cost_estimate=pl.CostEstimate(
            flops=8 * n * c * c, bytes_accessed=10 * n * c, transcendentals=n * c
        ),
        name="dx_part",
    )(pair, product, go, weights, norms, *chain)


def proj_kernel(step, pair, valid, w, norms, a, b, g_ga, g_pa, g_gb, g_pb, flip):
    cols, c = pair.shape[1:]

    def body(s, carry):
        hat, _ = layer_normalize(tile(pair, s, step).astype(F32))
        zn = (hat * norms[0:1] + norms[1:2]).astype(BF16)
        m = tile(valid, s, step).astype(F32)
        for at, d_gate, d_value in ((0, g_ga, g_pa), (2, g_gb, g_pb)):
            gate = sigmoid(dot(zn, w[at]))
            p = dot(zn, w[at + 1])
            mg = m * gate
            mgp = mg * p
            if at == 0:
                put(a, s, step, mgp)
            else:
                flip[pl.ds(s * step, step)] = mgp.reshape(step, cols, c)
            put(d_value, s, step, mg)
            put(d_gate, s, step, mgp * (1.0 - gate))
        return carry

    lax.fori_loop(0, pair.shape[0] // step, body, 0)
    b[...] = jnp.swapaxes(flip[...], 0, 1).astype(b.dtype)


def projections(pair, valid, weights, norms):
    rows, cols, c = pair.shape
    ib = 16 if rows % 16 == 0 else rows
    step = ib
    blk = pl.BlockSpec((ib, cols, c), lambda i: (i, 0, 0))
    swapped = pl.BlockSpec((cols, ib, c), lambda i: (0, i, 0))
    full = lambda shape: pl.BlockSpec(shape, lambda i: (0,) * len(shape))
    n = rows * cols
    kept = jax.ShapeDtypeStruct((rows, cols, c), BF16)
    return pl.pallas_call(
        functools.partial(proj_kernel, step),
        grid=(rows // ib,),
        in_specs=[blk, blk, full(weights.shape), full(norms.shape)],
        out_specs=[blk, swapped] + [blk] * 4,
        out_shape=[kept, jax.ShapeDtypeStruct((cols, rows, c), BF16)] + [kept] * 4,
        scratch_shapes=[pltpu.VMEM((ib, cols, c), F32)],
        compiler_params=pltpu.CompilerParams(vmem_limit_bytes=VMEM_LIMIT),
        cost_estimate=pl.CostEstimate(
            flops=8 * n * c * c, bytes_accessed=16 * n * c, transcendentals=2 * n * c
        ),
        name="projections",
    )(pair, valid, weights, norms)


def to_channels_kernel(slots, r, *refs):
    out = refs[-1]
    blocks = [ref[...].reshape(ref.shape[-3:]) for ref in refs[:-1]]
    x = jnp.concatenate(blocks, axis=1)
    out[...] = jnp.transpose(x, (2, 0, 1))


def to_channels(arrays, specs, r, lead, size, c):
    slots = len(specs)
    lanes = slots * size
    n = lead * lanes * c
    return pl.pallas_call(
        functools.partial(to_channels_kernel, slots),
        grid_spec=pltpu.PrefetchScalarGridSpec(
            num_scalar_prefetch=1,
            grid=(lead // 16,),
            in_specs=specs,
            out_specs=pl.BlockSpec((c, 16, lanes), lambda i, r: (0, i, 0)),
        ),
        out_shape=jax.ShapeDtypeStruct((c, lead, lanes), BF16),
        compiler_params=pltpu.CompilerParams(vmem_limit_bytes=VMEM_LIMIT),
        cost_estimate=pl.CostEstimate(flops=4 * n, bytes_accessed=4 * n, transcendentals=0),
        name="to_channels",
    )(r, *arrays)


def gathered_to_channels(g, r, at, size):
    n, rows, _, c = g.shape
    specs = [
        pl.BlockSpec((1, 16, size, c), lambda i, r, t=t: (r[0] ^ t, i, at, 0)) for t in range(n)
    ]
    return to_channels([g] * n, specs, r, rows, size, c)


def slots_to_channels(slots, r, off, size):
    lead, _, c = slots[0].shape
    specs = [pl.BlockSpec((16, size, c), lambda i, r: (i, off // size, 0))] * len(slots)
    return to_channels(slots, specs, r, lead, size, c)


def from_channels_kernel(slots, x, kept, sent):
    y = jnp.transpose(x[...], (1, 2, 0))
    size = y.shape[1] // slots
    for t in range(slots):
        out = sent if t % 2 else kept
        out[t // 2] = y[:, t * size : (t + 1) * size]


def from_channels(x, slots):
    c, lead, lanes = x.shape
    size = lanes // slots
    n = x.size
    out = pl.BlockSpec((slots // 2, 16, size, c), lambda i: (0, i, 0, 0))
    return pl.pallas_call(
        functools.partial(from_channels_kernel, slots),
        grid=(lead // 16,),
        in_specs=[pl.BlockSpec((c, 16, lanes), lambda i: (0, i, 0))],
        out_specs=[out, out],
        out_shape=[jax.ShapeDtypeStruct((slots // 2, lead, size, c), BF16)] * 2,
        compiler_params=pltpu.CompilerParams(vmem_limit_bytes=VMEM_LIMIT),
        cost_estimate=pl.CostEstimate(flops=4 * n, bytes_accessed=4 * n, transcendentals=0),
        name="from_channels",
    )(x)


def final_kernel(step, chained, pair, da, db0, db1, g_ga, g_pa, g_gb, g_pb, dol, wcat, norms, acc_in, *rest):
    gp, acc, flip = rest[-3:]
    c = pair.shape[-1]

    @pl.when(first_step(1))
    def _():
        acc[...] = acc_in[...]

    flip[...] = jnp.swapaxes(db0[...].astype(F32) + db1[...].astype(F32), 0, 1)

    def body(s, carry):
        hat, inv = layer_normalize(tile(pair, s, step).astype(F32))
        zn = (hat * norms[0:1] + norms[1:2]).astype(BF16)
        dav = tile(da, s, step).astype(F32)
        dbv = tile(flip, s, step)
        parts = [
            (dav * tile(g_ga, s, step).astype(F32)).astype(BF16),
            (dav * tile(g_pa, s, step).astype(F32)).astype(BF16),
            (dbv * tile(g_gb, s, step).astype(F32)).astype(BF16),
            (dbv * tile(g_pb, s, step).astype(F32)).astype(BF16),
            tile(dol, s, step),
        ]
        cat = jnp.concatenate(parts, axis=1)
        dzn = dot_t(cat, wcat[...])
        put(gp, s, step, layer_norm_backward(dzn * norms[0:1], hat, inv))
        grads = t_dot(zn, cat)
        for at in range(5):
            acc[at * c : (at + 1) * c] += grads[:, at * c : (at + 1) * c]
        acc[6 * c : 6 * c + 1] += jnp.sum(dzn * hat, axis=0, keepdims=True)
        acc[6 * c + 1 : 6 * c + 2] += jnp.sum(dzn, axis=0, keepdims=True)
        return carry

    lax.fori_loop(0, pair.shape[0] // step, body, 0)


def final_chunk(pair, da, db0, db1, gs, dol, wcat, norms, acc, off, size, chain):
    rows, cols, c = pair.shape
    ib = 16 if size % 16 == 0 else size
    step = ib
    base = off // ib
    blk = pl.BlockSpec((ib, cols, c), lambda i: (base + i, 0, 0))
    own = pl.BlockSpec((cols, ib, c), lambda i: (0, i, 0))
    full = lambda shape: pl.BlockSpec(shape, lambda i: (0,) * len(shape))
    n = size * cols
    return pl.pallas_call(
        functools.partial(final_kernel, step, bool(chain)),
        grid=(size // ib,),
        in_specs=[blk, blk, own, own]
        + [blk] * 5
        + [full(wcat.shape), full(norms.shape), full(acc.shape)]
        + ([pl.BlockSpec(memory_space=pl.ANY)] if chain else []),
        out_specs=[blk, full(acc.shape)],
        out_shape=[
            jax.ShapeDtypeStruct((rows, cols, c), BF16),
            jax.ShapeDtypeStruct(acc.shape, F32),
        ],
        input_output_aliases={12: 0} if chain else {},
        scratch_shapes=[pltpu.VMEM((ib, cols, c), F32)],
        compiler_params=pltpu.CompilerParams(vmem_limit_bytes=VMEM_LIMIT),
        cost_estimate=pl.CostEstimate(
            flops=20 * n * c * c, bytes_accessed=22 * n * c, transcendentals=n
        ),
        name="final_part",
    )(pair, da, db0, db1, *gs, dol, wcat, norms, acc, *chain)


def swap(v, axis, n, bit):
    return lax.ppermute(v, axis, [(r, r ^ bit) for r in range(n)])


def pick(v, at):
    return lax.dynamic_index_in_dim(v, at, 0, keepdims=False)


def bits_of(n):
    return [1 << k for k in range(n.bit_length() - 1)]


def gather_rows(v, n):
    slots = {0: v}
    for bit in bits_of(n)[::-1]:
        slots.update({t ^ bit: swap(x, "row", n, bit) for t, x in slots.items()})
    return [slots[t] for t in range(n)]


def reduce_rows(kept, sent, n):
    come = swap(sent, "row", n, 1)
    for bit in bits_of(n)[1:]:
        v = (kept.astype(F32) + come.astype(F32)).astype(BF16)
        v = v.reshape((-1, 2) + v.shape[1:])
        kept, come = v[:, 0], swap(v[:, 1], "row", n, bit)
    return kept[0], come[0]


def sum_all(v, n_row, n_col):
    steps = [("row", n_row, b) for b in bits_of(n_row)] + [("col", n_col, b) for b in bits_of(n_col)]
    halved = []
    for k, (axis, n, bit) in enumerate(steps):
        half = v.shape[0] // 2
        if 0 < k < len(steps) - 1 and v.shape[0] % 16 == 0:
            at = (lax.axis_index(axis) // bit) % 2
            pairs = v.reshape((2, half) + v.shape[1:])
            v = pick(pairs, at) + swap(pick(pairs, 1 - at), axis, n, bit)
            halved.append((axis, n, bit, at))
        else:
            v = v + swap(v, axis, n, bit)
    for axis, n, bit, at in halved[::-1]:
        got = swap(v, axis, n, bit)
        v = jnp.where(at == 0, jnp.concatenate([v, got]), jnp.concatenate([got, v]))
    return v


def triangles_plain(n_row, n_col, dx, a, b_swapped):
    rows, cols, c = dx.shape
    block = lax.all_gather(dx, "col", axis=1, tiled=True)
    b_all = lax.all_gather(b_swapped, "row", axis=1, tiled=True)
    part = jnp.einsum("ijc,ikc->kjc", block, a, preferred_element_type=F32).astype(BF16)
    db = lax.psum_scatter(part, "row", scatter_dimension=1, tiled=True)
    da = jnp.einsum("ijc,kjc->ikc", block, b_all, preferred_element_type=F32)
    return da.astype(BF16), [(db, jnp.zeros_like(db))], [(0, rows)]


def triangles(n, groups, size, a, b_swapped):
    r = lax.axis_index("row").astype(jnp.int32).reshape(1)
    b_slots = gather_rows(b_swapped, n)
    a_t = jnp.transpose(a, (2, 0, 1))
    major = Layout(major_to_minor=(0, 1, 2))
    da = None
    db, spans = [], []
    for group in groups:
        for at in range(group.shape[2] // size):
            off = len(spans) * size
            if da is not None:
                group, da = lax.optimization_barrier((group, da))
            dx_t = gathered_to_channels(group, r, at, size)
            part = jnp.einsum("cik,cij->ckj", a_t, dx_t, preferred_element_type=F32).astype(BF16)
            kept, sent = from_channels(part, n)
            db.append(reduce_rows(kept, sent, n))
            if da is None:
                dx_t, sent, *b_slots = lax.optimization_barrier((dx_t, sent, *b_slots))
            else:
                dx_t, sent = lax.optimization_barrier((dx_t, sent))
            b_t = slots_to_channels(b_slots, r, off, size)
            term = jnp.einsum("cij,ckj->cik", dx_t, b_t, preferred_element_type=F32)
            da = with_layout_constraint(term if da is None else da + term, major)
            spans.append((off, size))
    da = with_layout_constraint(da.astype(BF16), major)
    return jnp.transpose(da, (1, 2, 0)), db, spans


def shards(n_row, n_col, pair, product, mask, grad_out, weights, norms):
    rows, cols, c = pair.shape
    even = n_row == n_col and n_row & (n_row - 1) == 0 and cols % 32 == 0 and rows % 16 == 0
    size = 32 if even else cols
    widths = [size] * (cols // size)
    if len(widths) > 3:
        widths[1:3] = [2 * size]
    groups, chain, off = [], [], 0
    for width in widths:
        dx, *chain = dx_chunk(pair, product, grad_out, weights, norms, off, width, chain)
        groups.append(lax.all_gather(dx, "col", axis=0) if even else dx)
        if off == 0:
            valid = jnp.broadcast_to(mask.astype(BF16)[:, :, None], pair.shape)
            a, b_swapped, *gs = projections(pair, valid, weights, norms)
            chain[1], b_swapped = lax.optimization_barrier((chain[1], b_swapped))
        off += width
    dol, acc = chain
    if even:
        da, db, spans = triangles(n_row, groups, size, a, b_swapped)
    else:
        da, db, spans = triangles_plain(n_row, n_col, groups[0], a, b_swapped)
    wcat = jnp.transpose(weights[:5], (1, 0, 2)).reshape(c, 5 * c)
    chain = []
    for (db0, db1), (off, size) in zip(db, spans):
        grad_pair, acc = final_chunk(
            pair, da, db0, db1, gs, dol, wcat, norms, acc, off, size, chain
        )
        chain = [grad_pair]
    acc = sum_all(acc, n_row, n_col)
    return (grad_pair, acc[: 6 * c].reshape(6, c, c), acc[6 * c : 6 * c + 4])


def solution(mesh):
    in_specs = (
        P(("groups", "row"), "col", None),
        P(("groups", "row"), "col", None),
        P(("groups", "row"), "col"),
        P(("groups", "row"), "col", None),
        P(),
        P(),
    )
    out_specs = (P(("groups", "row"), "col", None), P("groups", None, None), P("groups", None))
    body = functools.partial(shards, mesh.shape["row"], mesh.shape["col"])
    return jax.shard_map(body, mesh=mesh, in_specs=in_specs, out_specs=out_specs, check_vma=False)
```

```python
import functools

import jax
import jax.numpy as jnp
from jax import lax
from jax.experimental import pallas as pl
from jax.experimental.layout import Layout, with_layout_constraint
from jax.experimental.pallas import tpu as pltpu
from jax.sharding import PartitionSpec as P

eps = 1e-05
F32 = jnp.float32
BF16 = jnp.bfloat16
VMEM_LIMIT = 48 * 1024 * 1024


def dot(x, y):
    return jnp.dot(x, y, preferred_element_type=F32)


def sigmoid(x):
    return 0.5 * jnp.tanh(0.5 * x) + 0.5


def dot_t(x, y):
    return lax.dot_general(x, y, (((1,), (1,)), ((), ())), preferred_element_type=F32)


def t_dot(x, y):
    return lax.dot_general(x, y, (((0,), (0,)), ((), ())), preferred_element_type=F32)


def layer_normalize(v):
    mean = jnp.mean(v, axis=-1, keepdims=True)
    cent = v - mean
    inv = lax.rsqrt(jnp.mean(cent * cent, axis=-1, keepdims=True) + eps)
    return cent * inv, inv


def layer_norm_backward(grad, hat, inv):
    return inv * (
        grad
        - jnp.mean(grad, axis=-1, keepdims=True)
        - hat * jnp.mean(grad * hat, axis=-1, keepdims=True)
    )


def tile(ref, s, step):
    block = ref[pl.ds(s * step, step)]
    return block.reshape(-1, block.shape[-1])


def put(ref, s, step, value):
    ref[pl.ds(s * step, step)] = value.reshape((step,) + ref.shape[1:]).astype(ref.dtype)


def first_step(axes):
    first = pl.program_id(0) == 0
    for axis in range(1, axes):
        first = jnp.logical_and(first, pl.program_id(axis) == 0)
    return first


def dx_kernel(step, chained, pair, product, go, w, norms, *rest):
    acc_in = rest[1] if chained else None
    dx, dol, acc = rest[-3:]
    c = pair.shape[-1]

    @pl.when(first_step(2))
    def _():
        acc[...] = acc_in[...] if chained else jnp.zeros_like(acc)

    def body(s, carry):
        hat, _ = layer_normalize(tile(pair, s, step).astype(F32))
        zn = (hat * norms[0:1] + norms[1:2]).astype(BF16)
        og = sigmoid(dot(zn, w[4]))
        xhat, inv2 = layer_normalize(tile(product, s, step).astype(F32))
        xn = (xhat * norms[2:3] + norms[3:4]).astype(BF16)
        y = dot(xn, w[5])
        gof = tile(go, s, step).astype(F32)
        d_y = (gof * og).astype(BF16)
        d_xn = dot_t(d_y, w[5])
        put(dx, s, step, layer_norm_backward(d_xn * norms[2:3], xhat, inv2))
        put(dol, s, step, gof * y * og * (1.0 - og))
        acc[5 * c : 6 * c] += t_dot(xn, d_y)
        acc[6 * c + 2 : 6 * c + 3] += jnp.sum(d_xn * xhat, axis=0, keepdims=True)
        acc[6 * c + 3 : 6 * c + 4] += jnp.sum(d_xn, axis=0, keepdims=True)
        return carry

    lax.fori_loop(0, pair.shape[0] // step, body, 0)


def dx_chunk(pair, product, go, weights, norms, off, size, chain):
    rows, cols, c = pair.shape
    jb = 16 if size % 16 == 0 else size
    ib = 80 if rows % 80 == 0 else rows // 2 if rows % 2 == 0 else rows
    step = 40 if ib % 40 == 0 else ib
    base = off // jb
    blk = pl.BlockSpec((ib, jb, c), lambda i, j: (i, base + j, 0))
    out = pl.BlockSpec((ib, jb, c), lambda i, j: (i, j, 0))
    full = lambda shape: pl.BlockSpec(shape, lambda i, j: (0,) * len(shape))
    n = rows * size
    acc = (6 * c + 32, c)
    return pl.pallas_call(
        functools.partial(dx_kernel, step, bool(chain)),
        grid=(rows // ib, size // jb),
        in_specs=[blk, blk, blk, full(weights.shape), full(norms.shape)]
        + ([pl.BlockSpec(memory_space=pl.ANY), full(acc)] if chain else []),
        out_specs=[out, blk, full(acc)],
        out_shape=[
            jax.ShapeDtypeStruct((rows, size, c), BF16),
            jax.ShapeDtypeStruct((rows, cols, c), BF16),
            jax.ShapeDtypeStruct(acc, F32),
        ],
        input_output_aliases={5: 1} if chain else {},
        compiler_params=pltpu.CompilerParams(vmem_limit_bytes=VMEM_LIMIT),
        cost_estimate=pl.CostEstimate(
            flops=8 * n * c * c, bytes_accessed=10 * n * c, transcendentals=n * c
        ),
        name="dx_part",
    )(pair, product, go, weights, norms, *chain)


def proj_kernel(step, pair, valid, w, norms, a, b, g_ga, g_pa, g_gb, g_pb, flip):
    cols, c = pair.shape[1:]

    def body(s, carry):
        hat, _ = layer_normalize(tile(pair, s, step).astype(F32))
        zn = (hat * norms[0:1] + norms[1:2]).astype(BF16)
        m = tile(valid, s, step).astype(F32)
        for at, d_gate, d_value in ((0, g_ga, g_pa), (2, g_gb, g_pb)):
            gate = sigmoid(dot(zn, w[at]))
            p = dot(zn, w[at + 1])
            mg = m * gate
            mgp = mg * p
            if at == 0:
                put(a, s, step, mgp)
            else:
                flip[pl.ds(s * step, step)] = mgp.reshape(step, cols, c)
            put(d_value, s, step, mg)
            put(d_gate, s, step, mgp * (1.0 - gate))
        return carry

    lax.fori_loop(0, pair.shape[0] // step, body, 0)
    b[...] = jnp.swapaxes(flip[...], 0, 1).astype(b.dtype)


def projections(pair, valid, weights, norms):
    rows, cols, c = pair.shape
    ib = 16 if rows % 16 == 0 else rows
    step = ib
    blk = pl.BlockSpec((ib, cols, c), lambda i: (i, 0, 0))
    swapped = pl.BlockSpec((cols, ib, c), lambda i: (0, i, 0))
    full = lambda shape: pl.BlockSpec(shape, lambda i: (0,) * len(shape))
    n = rows * cols
    kept = jax.ShapeDtypeStruct((rows, cols, c), BF16)
    return pl.pallas_call(
        functools.partial(proj_kernel, step),
        grid=(rows // ib,),
        in_specs=[blk, blk, full(weights.shape), full(norms.shape)],
        out_specs=[blk, swapped] + [blk] * 4,
        out_shape=[kept, jax.ShapeDtypeStruct((cols, rows, c), BF16)] + [kept] * 4,
        scratch_shapes=[pltpu.VMEM((ib, cols, c), F32)],
        compiler_params=pltpu.CompilerParams(vmem_limit_bytes=VMEM_LIMIT),
        cost_estimate=pl.CostEstimate(
            flops=8 * n * c * c, bytes_accessed=16 * n * c, transcendentals=2 * n * c
        ),
        name="projections",
    )(pair, valid, weights, norms)


def to_channels_kernel(slots, r, *refs):
    out = refs[-1]
    blocks = [ref[...].reshape(ref.shape[-3:]) for ref in refs[:-1]]
    x = jnp.concatenate(blocks, axis=1)
    out[...] = jnp.transpose(x, (2, 0, 1))


def to_channels(arrays, specs, r, lead, size, c):
    slots = len(specs)
    lanes = slots * size
    n = lead * lanes * c
    return pl.pallas_call(
        functools.partial(to_channels_kernel, slots),
        grid_spec=pltpu.PrefetchScalarGridSpec(
            num_scalar_prefetch=1,
            grid=(lead // 16,),
            in_specs=specs,
            out_specs=pl.BlockSpec((c, 16, lanes), lambda i, r: (0, i, 0)),
        ),
        out_shape=jax.ShapeDtypeStruct((c, lead, lanes), BF16),
        compiler_params=pltpu.CompilerParams(vmem_limit_bytes=VMEM_LIMIT),
        cost_estimate=pl.CostEstimate(flops=4 * n, bytes_accessed=4 * n, transcendentals=0),
        name="to_channels",
    )(r, *arrays)


def gathered_to_channels(g, r, at, size):
    n, rows, _, c = g.shape
    specs = [
        pl.BlockSpec((1, 16, size, c), lambda i, r, t=t: (r[0] ^ t, i, at, 0)) for t in range(n)
    ]
    return to_channels([g] * n, specs, r, rows, size, c)


def slots_to_channels(slots, r, off, size):
    lead, _, c = slots[0].shape
    specs = [pl.BlockSpec((16, size, c), lambda i, r: (i, off // size, 0))] * len(slots)
    return to_channels(slots, specs, r, lead, size, c)


def from_channels_kernel(slots, x, kept, sent):
    y = jnp.transpose(x[...], (1, 2, 0))
    size = y.shape[1] // slots
    for t in range(slots):
        out = sent if t % 2 else kept
        out[t // 2] = y[:, t * size : (t + 1) * size]


def from_channels(x, slots):
    c, lead, lanes = x.shape
    size = lanes // slots
    n = x.size
    out = pl.BlockSpec((slots // 2, 16, size, c), lambda i: (0, i, 0, 0))
    return pl.pallas_call(
        functools.partial(from_channels_kernel, slots),
        grid=(lead // 16,),
        in_specs=[pl.BlockSpec((c, 16, lanes), lambda i: (0, i, 0))],
        out_specs=[out, out],
        out_shape=[jax.ShapeDtypeStruct((slots // 2, lead, size, c), BF16)] * 2,
        compiler_params=pltpu.CompilerParams(vmem_limit_bytes=VMEM_LIMIT),
        cost_estimate=pl.CostEstimate(flops=4 * n, bytes_accessed=4 * n, transcendentals=0),
        name="from_channels",
    )(x)


def final_kernel(step, chained, pair, da, db0, db1, g_ga, g_pa, g_gb, g_pb, dol, wcat, norms, acc_in, *rest):
    gp, acc, flip = rest[-3:]
    c = pair.shape[-1]

    @pl.when(first_step(1))
    def _():
        acc[...] = acc_in[...]

    flip[...] = jnp.swapaxes(db0[...].astype(F32) + db1[...].astype(F32), 0, 1)

    def body(s, carry):
        hat, inv = layer_normalize(tile(pair, s, step).astype(F32))
        zn = (hat * norms[0:1] + norms[1:2]).astype(BF16)
        dav = tile(da, s, step).astype(F32)
        dbv = tile(flip, s, step)
        parts = [
            (dav * tile(g_ga, s, step).astype(F32)).astype(BF16),
            (dav * tile(g_pa, s, step).astype(F32)).astype(BF16),
            (dbv * tile(g_gb, s, step).astype(F32)).astype(BF16),
            (dbv * tile(g_pb, s, step).astype(F32)).astype(BF16),
            tile(dol, s, step),
        ]
        cat = jnp.concatenate(parts, axis=1)
        dzn = dot_t(cat, wcat[...])
        put(gp, s, step, layer_norm_backward(dzn * norms[0:1], hat, inv))
        grads = t_dot(zn, cat)
        for at in range(5):
            acc[at * c : (at + 1) * c] += grads[:, at * c : (at + 1) * c]
        acc[6 * c : 6 * c + 1] += jnp.sum(dzn * hat, axis=0, keepdims=True)
        acc[6 * c + 1 : 6 * c + 2] += jnp.sum(dzn, axis=0, keepdims=True)
        return carry

    lax.fori_loop(0, pair.shape[0] // step, body, 0)


def final_chunk(pair, da, db0, db1, gs, dol, wcat, norms, acc, off, size, chain):
    rows, cols, c = pair.shape
    ib = 16 if size % 16 == 0 else size
    step = ib
    base = off // ib
    blk = pl.BlockSpec((ib, cols, c), lambda i: (base + i, 0, 0))
    own = pl.BlockSpec((cols, ib, c), lambda i: (0, i, 0))
    full = lambda shape: pl.BlockSpec(shape, lambda i: (0,) * len(shape))
    n = size * cols
    return pl.pallas_call(
        functools.partial(final_kernel, step, bool(chain)),
        grid=(size // ib,),
        in_specs=[blk, blk, own, own]
        + [blk] * 5
        + [full(wcat.shape), full(norms.shape), full(acc.shape)]
        + ([pl.BlockSpec(memory_space=pl.ANY)] if chain else []),
        out_specs=[blk, full(acc.shape)],
        out_shape=[
            jax.ShapeDtypeStruct((rows, cols, c), BF16),
            jax.ShapeDtypeStruct(acc.shape, F32),
        ],
        input_output_aliases={12: 0} if chain else {},
        scratch_shapes=[pltpu.VMEM((ib, cols, c), F32)],
        compiler_params=pltpu.CompilerParams(vmem_limit_bytes=VMEM_LIMIT),
        cost_estimate=pl.CostEstimate(
            flops=20 * n * c * c, bytes_accessed=22 * n * c, transcendentals=n
        ),
        name="final_part",
    )(pair, da, db0, db1, *gs, dol, wcat, norms, acc, *chain)


def swap(v, axis, n, bit):
    return lax.ppermute(v, axis, [(r, r ^ bit) for r in range(n)])


def pick(v, at):
    return lax.dynamic_index_in_dim(v, at, 0, keepdims=False)


def bits_of(n):
    return [1 << k for k in range(n.bit_length() - 1)]


def gather_rows(v, n):
    slots = {0: v}
    for bit in bits_of(n)[::-1]:
        slots.update({t ^ bit: swap(x, "row", n, bit) for t, x in slots.items()})
    return [slots[t] for t in range(n)]


def reduce_cores(kept, sent, n):
    come = swap(sent, "row", n, 1)
    if n == 2:
        return kept, come
    return (kept.astype(F32) + come.astype(F32)).astype(BF16), None


def reduce_chips(v, come, n):
    if come is not None:
        return v[0], come[0]
    for bit in bits_of(n)[1:]:
        v = v.reshape((-1, 2) + v.shape[1:])
        kept, come = v[:, 0], swap(v[:, 1], "row", n, bit)
        v = (kept.astype(F32) + come.astype(F32)).astype(BF16)
    return kept[0], come[0]


def sum_all(v, n_row, n_col):
    steps = [("row", n_row, b) for b in bits_of(n_row)] + [("col", n_col, b) for b in bits_of(n_col)]
    halved = []
    for k, (axis, n, bit) in enumerate(steps):
        half = v.shape[0] // 2
        if 0 < k < len(steps) - 1 and v.shape[0] % 16 == 0:
            at = (lax.axis_index(axis) // bit) % 2
            pairs = v.reshape((2, half) + v.shape[1:])
            v = pick(pairs, at) + swap(pick(pairs, 1 - at), axis, n, bit)
            halved.append((axis, n, bit, at))
        else:
            v = v + swap(v, axis, n, bit)
    for axis, n, bit, at in halved[::-1]:
        got = swap(v, axis, n, bit)
        v = jnp.where(at == 0, jnp.concatenate([v, got]), jnp.concatenate([got, v]))
    return v


def triangles_plain(n_row, n_col, dx, a, b_swapped):
    rows, cols, c = dx.shape
    block = lax.all_gather(dx, "col", axis=1, tiled=True)
    b_all = lax.all_gather(b_swapped, "row", axis=1, tiled=True)
    part = jnp.einsum("ijc,ikc->kjc", block, a, preferred_element_type=F32).astype(BF16)
    db = lax.psum_scatter(part, "row", scatter_dimension=1, tiled=True)
    da = jnp.einsum("ijc,kjc->ikc", block, b_all, preferred_element_type=F32)
    return da.astype(BF16), [(db, jnp.zeros_like(db))], [(0, rows)]


def triangles(n, groups, size, a, b_swapped):
    r = lax.axis_index("row").astype(jnp.int32).reshape(1)
    b_slots = gather_rows(b_swapped, n)
    a_t = jnp.transpose(a, (2, 0, 1))
    major = Layout(major_to_minor=(0, 1, 2))
    da, b_t = None, None
    db, spans = [], []
    for group in groups:
        for at in range(group.shape[2] // size):
            off = len(spans) * size
            if da is not None:
                b_t = slots_to_channels(b_slots, r, off, size)
                group, da, b_t = lax.optimization_barrier((group, da, b_t))
            dx_t = gathered_to_channels(group, r, at, size)
            part = jnp.einsum("cik,cij->ckj", a_t, dx_t, preferred_element_type=F32).astype(BF16)
            kept, sent = from_channels(part, n)
            half, come = reduce_cores(kept, sent, n)
            if da is None:
                dx_t, sent, *b_slots = lax.optimization_barrier((dx_t, sent, *b_slots))
                b_t = slots_to_channels(b_slots, r, off, size)
            else:
                dx_t, sent = lax.optimization_barrier((dx_t, sent))
            term = jnp.einsum("cij,ckj->cik", dx_t, b_t, preferred_element_type=F32)
            da = with_layout_constraint(term if da is None else da + term, major)
            da, half = lax.optimization_barrier((da, half))
            db.append(reduce_chips(half, come, n))
            spans.append((off, size))
    da = with_layout_constraint(da.astype(BF16), major)
    return jnp.transpose(da, (1, 2, 0)), db, spans


def shards(n_row, n_col, pair, product, mask, grad_out, weights, norms):
    rows, cols, c = pair.shape
    even = n_row == n_col and n_row & (n_row - 1) == 0 and cols % 32 == 0 and rows % 16 == 0
    size = 32 if even else cols
    widths = [size] * (cols // size)
    if len(widths) > 3:
        widths[1:3] = [2 * size]
    groups, chain, off = [], [], 0
    for width in widths:
        dx, *chain = dx_chunk(pair, product, grad_out, weights, norms, off, width, chain)
        groups.append(lax.all_gather(dx, "col", axis=0) if even else dx)
        if off == 0:
            valid = jnp.broadcast_to(mask.astype(BF16)[:, :, None], pair.shape)
            a, b_swapped, *gs = projections(pair, valid, weights, norms)
            chain[1], b_swapped = lax.optimization_barrier((chain[1], b_swapped))
        off += width
    dol, acc = chain
    if even:
        da, db, spans = triangles(n_row, groups, size, a, b_swapped)
    else:
        da, db, spans = triangles_plain(n_row, n_col, groups[0], a, b_swapped)
    wcat = jnp.transpose(weights[:5], (1, 0, 2)).reshape(c, 5 * c)
    chain = []
    for (db0, db1), (off, size) in zip(db, spans):
        grad_pair, acc = final_chunk(
            pair, da, db0, db1, gs, dol, wcat, norms, acc, off, size, chain
        )
        chain = [grad_pair]
    acc = sum_all(acc, n_row, n_col)
    return (grad_pair, acc[: 6 * c].reshape(6, c, c), acc[6 * c : 6 * c + 4])


def solution(mesh):
    in_specs = (
        P(("groups", "row"), "col", None),
        P(("groups", "row"), "col", None),
        P(("groups", "row"), "col"),
        P(("groups", "row"), "col", None),
        P(),
        P(),
    )
    out_specs = (P(("groups", "row"), "col", None), P("groups", None, None), P("groups", None))
    body = functools.partial(shards, mesh.shape["row"], mesh.shape["col"])
    return jax.shard_map(body, mesh=mesh, in_specs=in_specs, out_specs=out_specs, check_vma=False)
```

```python
import functools

import jax
import jax.numpy as jnp
from jax import lax
from jax.experimental import pallas as pl
from jax.experimental.layout import Layout, with_layout_constraint
from jax.experimental.pallas import tpu as pltpu
from jax.sharding import PartitionSpec as P

eps = 1e-05
F32 = jnp.float32
BF16 = jnp.bfloat16
VMEM_LIMIT = 48 * 1024 * 1024


def dot(x, y):
    return jnp.dot(x, y, preferred_element_type=F32)


def sigmoid(x):
    return 0.5 * jnp.tanh(0.5 * x) + 0.5


def dot_t(x, y):
    return lax.dot_general(x, y, (((1,), (1,)), ((), ())), preferred_element_type=F32)


def t_dot(x, y):
    return lax.dot_general(x, y, (((0,), (0,)), ((), ())), preferred_element_type=F32)


def layer_normalize(v):
    mean = jnp.mean(v, axis=-1, keepdims=True)
    cent = v - mean
    inv = lax.rsqrt(jnp.mean(cent * cent, axis=-1, keepdims=True) + eps)
    return cent * inv, inv


def layer_norm_backward(grad, hat, inv):
    return inv * (
        grad
        - jnp.mean(grad, axis=-1, keepdims=True)
        - hat * jnp.mean(grad * hat, axis=-1, keepdims=True)
    )


def tile(ref, s, step):
    block = ref[pl.ds(s * step, step)]
    return block.reshape(-1, block.shape[-1])


def put(ref, s, step, value):
    ref[pl.ds(s * step, step)] = value.reshape((step,) + ref.shape[1:]).astype(ref.dtype)


def first_step(axes):
    first = pl.program_id(0) == 0
    for axis in range(1, axes):
        first = jnp.logical_and(first, pl.program_id(axis) == 0)
    return first


def dx_kernel(step, chained, pair, product, go, w, norms, *rest):
    acc_in = rest[1] if chained else None
    dx, dol, acc = rest[-3:]
    c = pair.shape[-1]

    @pl.when(first_step(2))
    def _():
        acc[...] = acc_in[...] if chained else jnp.zeros_like(acc)

    def body(s, carry):
        hat, _ = layer_normalize(tile(pair, s, step).astype(F32))
        zn = (hat * norms[0:1] + norms[1:2]).astype(BF16)
        og = sigmoid(dot(zn, w[4]))
        xhat, inv2 = layer_normalize(tile(product, s, step).astype(F32))
        xn = (xhat * norms[2:3] + norms[3:4]).astype(BF16)
        y = dot(xn, w[5])
        gof = tile(go, s, step).astype(F32)
        d_y = (gof * og).astype(BF16)
        d_xn = dot_t(d_y, w[5])
        put(dx, s, step, layer_norm_backward(d_xn * norms[2:3], xhat, inv2))
        put(dol, s, step, gof * y * og * (1.0 - og))
        acc[5 * c : 6 * c] += t_dot(xn, d_y)
        acc[6 * c + 2 : 6 * c + 3] += jnp.sum(d_xn * xhat, axis=0, keepdims=True)
        acc[6 * c + 3 : 6 * c + 4] += jnp.sum(d_xn, axis=0, keepdims=True)
        return carry

    lax.fori_loop(0, pair.shape[0] // step, body, 0)


def dx_chunk(pair, product, go, weights, norms, off, size, chain):
    rows, cols, c = pair.shape
    jb = 16 if size % 16 == 0 else size
    ib = 80 if rows % 80 == 0 else rows // 2 if rows % 2 == 0 else rows
    step = 40 if ib % 40 == 0 else ib
    base = off // jb
    blk = pl.BlockSpec((ib, jb, c), lambda i, j: (i, base + j, 0))
    out = pl.BlockSpec((ib, jb, c), lambda i, j: (i, j, 0))
    full = lambda shape: pl.BlockSpec(shape, lambda i, j: (0,) * len(shape))
    n = rows * size
    acc = (6 * c + 32, c)
    return pl.pallas_call(
        functools.partial(dx_kernel, step, bool(chain)),
        grid=(rows // ib, size // jb),
        in_specs=[blk, blk, blk, full(weights.shape), full(norms.shape)]
        + ([pl.BlockSpec(memory_space=pl.ANY), full(acc)] if chain else []),
        out_specs=[out, blk, full(acc)],
        out_shape=[
            jax.ShapeDtypeStruct((rows, size, c), BF16),
            jax.ShapeDtypeStruct((rows, cols, c), BF16),
            jax.ShapeDtypeStruct(acc, F32),
        ],
        input_output_aliases={5: 1} if chain else {},
        compiler_params=pltpu.CompilerParams(vmem_limit_bytes=VMEM_LIMIT),
        cost_estimate=pl.CostEstimate(
            flops=8 * n * c * c, bytes_accessed=10 * n * c, transcendentals=n * c
        ),
        name="dx_part",
    )(pair, product, go, weights, norms, *chain)


def proj_kernel(step, pair, valid, w, norms, a, b, g_ga, g_pa, g_gb, g_pb, flip):
    cols, c = pair.shape[1:]

    def body(s, carry):
        hat, _ = layer_normalize(tile(pair, s, step).astype(F32))
        zn = (hat * norms[0:1] + norms[1:2]).astype(BF16)
        m = tile(valid, s, step).astype(F32)
        for at, d_gate, d_value in ((0, g_ga, g_pa), (2, g_gb, g_pb)):
            gate = sigmoid(dot(zn, w[at]))
            p = dot(zn, w[at + 1])
            mg = m * gate
            mgp = mg * p
            if at == 0:
                put(a, s, step, mgp)
            else:
                flip[pl.ds(s * step, step)] = mgp.reshape(step, cols, c)
            put(d_value, s, step, mg)
            put(d_gate, s, step, mgp * (1.0 - gate))
        return carry

    lax.fori_loop(0, pair.shape[0] // step, body, 0)
    b[...] = jnp.swapaxes(flip[...], 0, 1).astype(b.dtype)


def projections(pair, valid, weights, norms):
    rows, cols, c = pair.shape
    ib = 16 if rows % 16 == 0 else rows
    step = ib
    blk = pl.BlockSpec((ib, cols, c), lambda i: (i, 0, 0))
    swapped = pl.BlockSpec((cols, ib, c), lambda i: (0, i, 0))
    full = lambda shape: pl.BlockSpec(shape, lambda i: (0,) * len(shape))
    n = rows * cols
    kept = jax.ShapeDtypeStruct((rows, cols, c), BF16)
    return pl.pallas_call(
        functools.partial(proj_kernel, step),
        grid=(rows // ib,),
        in_specs=[blk, blk, full(weights.shape), full(norms.shape)],
        out_specs=[blk, swapped] + [blk] * 4,
        out_shape=[kept, jax.ShapeDtypeStruct((cols, rows, c), BF16)] + [kept] * 4,
        scratch_shapes=[pltpu.VMEM((ib, cols, c), F32)],
        compiler_params=pltpu.CompilerParams(vmem_limit_bytes=VMEM_LIMIT),
        cost_estimate=pl.CostEstimate(
            flops=8 * n * c * c, bytes_accessed=16 * n * c, transcendentals=2 * n * c
        ),
        name="projections",
    )(pair, valid, weights, norms)


def to_channels_kernel(slots, r, *refs):
    out = refs[-1]
    blocks = [ref[...].reshape(ref.shape[-3:]) for ref in refs[:-1]]
    x = jnp.concatenate(blocks, axis=1)
    out[...] = jnp.transpose(x, (2, 0, 1))


def to_channels(arrays, specs, r, lead, size, c):
    slots = len(specs)
    lanes = slots * size
    n = lead * lanes * c
    return pl.pallas_call(
        functools.partial(to_channels_kernel, slots),
        grid_spec=pltpu.PrefetchScalarGridSpec(
            num_scalar_prefetch=1,
            grid=(lead // 16,),
            in_specs=specs,
            out_specs=pl.BlockSpec((c, 16, lanes), lambda i, r: (0, i, 0)),
        ),
        out_shape=jax.ShapeDtypeStruct((c, lead, lanes), BF16),
        compiler_params=pltpu.CompilerParams(vmem_limit_bytes=VMEM_LIMIT),
        cost_estimate=pl.CostEstimate(flops=4 * n, bytes_accessed=4 * n, transcendentals=0),
        name="to_channels",
    )(r, *arrays)


def gathered_to_channels(g, r, at, size):
    n, rows, _, c = g.shape
    specs = [
        pl.BlockSpec((1, 16, size, c), lambda i, r, t=t: (r[0] ^ t, i, at, 0)) for t in range(n)
    ]
    return to_channels([g] * n, specs, r, rows, size, c)


def slots_to_channels(slots, r, off, size):
    lead, _, c = slots[0].shape
    specs = [pl.BlockSpec((16, size, c), lambda i, r: (i, off // size, 0))] * len(slots)
    return to_channels(slots, specs, r, lead, size, c)


def from_channels_kernel(slots, x, kept, sent):
    y = jnp.transpose(x[...], (1, 2, 0))
    size = y.shape[1] // slots
    for t in range(slots):
        out = sent if t % 2 else kept
        out[t // 2] = y[:, t * size : (t + 1) * size]


def from_channels(x, slots):
    c, lead, lanes = x.shape
    size = lanes // slots
    n = x.size
    out = pl.BlockSpec((slots // 2, 16, size, c), lambda i: (0, i, 0, 0))
    return pl.pallas_call(
        functools.partial(from_channels_kernel, slots),
        grid=(lead // 16,),
        in_specs=[pl.BlockSpec((c, 16, lanes), lambda i: (0, i, 0))],
        out_specs=[out, out],
        out_shape=[jax.ShapeDtypeStruct((slots // 2, lead, size, c), BF16)] * 2,
        compiler_params=pltpu.CompilerParams(vmem_limit_bytes=VMEM_LIMIT),
        cost_estimate=pl.CostEstimate(flops=4 * n, bytes_accessed=4 * n, transcendentals=0),
        name="from_channels",
    )(x)


def final_kernel(step, chained, pair, da, db0, db1, g_ga, g_pa, g_gb, g_pb, dol, wcat, norms, acc_in, *rest):
    gp, acc, flip = rest[-3:]
    c = pair.shape[-1]

    @pl.when(first_step(1))
    def _():
        acc[...] = acc_in[...]

    flip[...] = jnp.swapaxes(db0[...].astype(F32) + db1[...].astype(F32), 0, 1)

    def body(s, carry):
        hat, inv = layer_normalize(tile(pair, s, step).astype(F32))
        zn = (hat * norms[0:1] + norms[1:2]).astype(BF16)
        dav = tile(da, s, step).astype(F32)
        dbv = tile(flip, s, step)
        parts = [
            (dav * tile(g_ga, s, step).astype(F32)).astype(BF16),
            (dav * tile(g_pa, s, step).astype(F32)).astype(BF16),
            (dbv * tile(g_gb, s, step).astype(F32)).astype(BF16),
            (dbv * tile(g_pb, s, step).astype(F32)).astype(BF16),
            tile(dol, s, step),
        ]
        cat = jnp.concatenate(parts, axis=1)
        dzn = dot_t(cat, wcat[...])
        put(gp, s, step, layer_norm_backward(dzn * norms[0:1], hat, inv))
        grads = t_dot(zn, cat)
        for at in range(5):
            acc[at * c : (at + 1) * c] += grads[:, at * c : (at + 1) * c]
        acc[6 * c : 6 * c + 1] += jnp.sum(dzn * hat, axis=0, keepdims=True)
        acc[6 * c + 1 : 6 * c + 2] += jnp.sum(dzn, axis=0, keepdims=True)
        return carry

    lax.fori_loop(0, pair.shape[0] // step, body, 0)


def final_chunk(pair, da, db0, db1, gs, dol, wcat, norms, acc, off, size, chain):
    rows, cols, c = pair.shape
    ib = 16 if size % 16 == 0 else size
    step = ib
    base = off // ib
    blk = pl.BlockSpec((ib, cols, c), lambda i: (base + i, 0, 0))
    own = pl.BlockSpec((cols, ib, c), lambda i: (0, i, 0))
    full = lambda shape: pl.BlockSpec(shape, lambda i: (0,) * len(shape))
    n = size * cols
    return pl.pallas_call(
        functools.partial(final_kernel, step, bool(chain)),
        grid=(size // ib,),
        in_specs=[blk, blk, own, own]
        + [blk] * 5
        + [full(wcat.shape), full(norms.shape), full(acc.shape)]
        + ([pl.BlockSpec(memory_space=pl.ANY)] if chain else []),
        out_specs=[blk, full(acc.shape)],
        out_shape=[
            jax.ShapeDtypeStruct((rows, cols, c), BF16),
            jax.ShapeDtypeStruct(acc.shape, F32),
        ],
        input_output_aliases={12: 0} if chain else {},
        scratch_shapes=[pltpu.VMEM((ib, cols, c), F32)],
        compiler_params=pltpu.CompilerParams(vmem_limit_bytes=VMEM_LIMIT),
        cost_estimate=pl.CostEstimate(
            flops=20 * n * c * c, bytes_accessed=22 * n * c, transcendentals=n
        ),
        name="final_part",
    )(pair, da, db0, db1, *gs, dol, wcat, norms, acc, *chain)


def swap(v, axis, n, bit):
    return lax.ppermute(v, axis, [(r, r ^ bit) for r in range(n)])


def pick(v, at):
    return lax.dynamic_index_in_dim(v, at, 0, keepdims=False)


def bits_of(n):
    return [1 << k for k in range(n.bit_length() - 1)]


def chip_slots(v, n):
    slots = {0: v}
    for bit in bits_of(n)[:0:-1]:
        slots.update({t ^ bit: swap(x, "row", n, bit) for t, x in slots.items()})
    return [slots[t] for t in range(0, n, 2)]


def core_slots(slots, n):
    return [x for v in slots for x in (v, swap(v, "row", n, 1))]


def reduce_cores(kept, sent, n):
    come = swap(sent, "row", n, 1)
    if n == 2:
        return kept, come
    return (kept.astype(F32) + come.astype(F32)).astype(BF16), None


def reduce_chips(v, come, n):
    if come is not None:
        return v[0], come[0]
    for bit in bits_of(n)[1:]:
        v = v.reshape((-1, 2) + v.shape[1:])
        kept, come = v[:, 0], swap(v[:, 1], "row", n, bit)
        v = (kept.astype(F32) + come.astype(F32)).astype(BF16)
    return kept[0], come[0]


def sum_all(v, n_row, n_col):
    steps = [("row", n_row, b) for b in bits_of(n_row)] + [("col", n_col, b) for b in bits_of(n_col)]
    halved = []
    for k, (axis, n, bit) in enumerate(steps):
        half = v.shape[0] // 2
        if 0 < k < len(steps) - 1 and v.shape[0] % 16 == 0:
            at = (lax.axis_index(axis) // bit) % 2
            pairs = v.reshape((2, half) + v.shape[1:])
            v = pick(pairs, at) + swap(pick(pairs, 1 - at), axis, n, bit)
            halved.append((axis, n, bit, at))
        else:
            v = v + swap(v, axis, n, bit)
    for axis, n, bit, at in halved[::-1]:
        got = swap(v, axis, n, bit)
        v = jnp.where(at == 0, jnp.concatenate([v, got]), jnp.concatenate([got, v]))
    return v


def triangles_plain(n_row, n_col, dx, a, b_swapped):
    rows, cols, c = dx.shape
    block = lax.all_gather(dx, "col", axis=1, tiled=True)
    b_all = lax.all_gather(b_swapped, "row", axis=1, tiled=True)
    part = jnp.einsum("ijc,ikc->kjc", block, a, preferred_element_type=F32).astype(BF16)
    db = lax.psum_scatter(part, "row", scatter_dimension=1, tiled=True)
    da = jnp.einsum("ijc,kjc->ikc", block, b_all, preferred_element_type=F32)
    return da.astype(BF16), [(db, jnp.zeros_like(db))], [(0, rows)]


def triangles(n, groups, size, a, b_swapped, acc):
    r = lax.axis_index("row").astype(jnp.int32).reshape(1)
    cols = b_swapped.shape[1]
    split = 2 * size if cols > 2 * size else cols
    early = chip_slots(b_swapped[:, :split], n)
    late = chip_slots(b_swapped[:, split:], n) if split < cols else []
    a_t = jnp.transpose(a, (2, 0, 1))
    first, a_t, acc = lax.optimization_barrier((groups[0], a_t, acc))
    groups = [first] + groups[1:]
    major = Layout(major_to_minor=(0, 1, 2))
    da, b_t = None, None
    db, spans = [], []
    for group in groups:
        for at in range(group.shape[2] // size):
            q = len(spans)
            off = q * size
            if q > 0:
                slots, start = (b_early, off) if off < split else (b_late, off - split)
                b_t = slots_to_channels(slots, r, start, size)
                group, da, b_t = lax.optimization_barrier((group, da, b_t))
            dx_t = gathered_to_channels(group, r, at, size)
            part = jnp.einsum("cik,cij->ckj", a_t, dx_t, preferred_element_type=F32).astype(BF16)
            kept, sent = from_channels(part, n)
            if q == 0:
                dx_t, kept, sent, *early = lax.optimization_barrier((dx_t, kept, sent, *early))
                b_early = core_slots(early, n)
                b_t = slots_to_channels(b_early, r, off, size)
            else:
                dx_t, kept, sent = lax.optimization_barrier((dx_t, kept, sent))
            half, come = reduce_cores(kept, sent, n)
            term = jnp.einsum("cij,ckj->cik", dx_t, b_t, preferred_element_type=F32)
            da = with_layout_constraint(term if q == 0 else da + term, major)
            if q == 0:
                da, half, *late = lax.optimization_barrier((da, half, *late))
                b_late = core_slots(late, n)
            else:
                da, half, db[-1][1] = lax.optimization_barrier((da, half, db[-1][1]))
            db.append(list(reduce_chips(half, come, n)))
            spans.append((off, size))
    da = with_layout_constraint(da.astype(BF16), major)
    return jnp.transpose(da, (1, 2, 0)), db, spans, acc


def shards(n_row, n_col, pair, product, mask, grad_out, weights, norms):
    rows, cols, c = pair.shape
    even = n_row == n_col and n_row & (n_row - 1) == 0 and cols % 32 == 0 and rows % 16 == 0
    size = 32 if even else cols
    widths = [size] * (cols // size)
    if len(widths) > 3:
        widths[1:3] = [2 * size]
    groups, chain, off = [], [], 0
    for width in widths:
        dx, *chain = dx_chunk(pair, product, grad_out, weights, norms, off, width, chain)
        groups.append(lax.all_gather(dx, "col", axis=0) if even else dx)
        if off == 0:
            valid = jnp.broadcast_to(mask.astype(BF16)[:, :, None], pair.shape)
            a, b_swapped, *gs = projections(pair, valid, weights, norms)
            chain[1], b_swapped = lax.optimization_barrier((chain[1], b_swapped))
        off += width
    dol, acc = chain
    if even:
        da, db, spans, acc = triangles(n_row, groups, size, a, b_swapped, acc)
    else:
        da, db, spans = triangles_plain(n_row, n_col, groups[0], a, b_swapped)
    wcat = jnp.transpose(weights[:5], (1, 0, 2)).reshape(c, 5 * c)
    chain = []
    for (db0, db1), (off, size) in zip(db, spans):
        grad_pair, acc = final_chunk(
            pair, da, db0, db1, gs, dol, wcat, norms, acc, off, size, chain
        )
        chain = [grad_pair]
    acc = sum_all(acc, n_row, n_col)
    return (grad_pair, acc[: 6 * c].reshape(6, c, c), acc[6 * c : 6 * c + 4])


def solution(mesh):
    in_specs = (
        P(("groups", "row"), "col", None),
        P(("groups", "row"), "col", None),
        P(("groups", "row"), "col"),
        P(("groups", "row"), "col", None),
        P(),
        P(),
    )
    out_specs = (P(("groups", "row"), "col", None), P("groups", None, None), P("groups", None))
    body = functools.partial(shards, mesh.shape["row"], mesh.shape["col"])
    return jax.shard_map(body, mesh=mesh, in_specs=in_specs, out_specs=out_specs, check_vma=False)
```

```python
import functools

import jax
import jax.numpy as jnp
from jax import lax
from jax.experimental import pallas as pl
from jax.experimental.layout import Layout, with_layout_constraint
from jax.experimental.pallas import tpu as pltpu
from jax.sharding import PartitionSpec as P

eps = 1e-05
F32 = jnp.float32
BF16 = jnp.bfloat16
VMEM_LIMIT = 48 * 1024 * 1024


def dot(x, y):
    return jnp.dot(x, y, preferred_element_type=F32)


def sigmoid(x):
    return 0.5 * jnp.tanh(0.5 * x) + 0.5


def dot_t(x, y):
    return lax.dot_general(x, y, (((1,), (1,)), ((), ())), preferred_element_type=F32)


def t_dot(x, y):
    return lax.dot_general(x, y, (((0,), (0,)), ((), ())), preferred_element_type=F32)


def layer_normalize(v):
    mean = jnp.mean(v, axis=-1, keepdims=True)
    cent = v - mean
    inv = lax.rsqrt(jnp.mean(cent * cent, axis=-1, keepdims=True) + eps)
    return cent * inv, inv


def layer_norm_backward(grad, hat, inv):
    return inv * (
        grad
        - jnp.mean(grad, axis=-1, keepdims=True)
        - hat * jnp.mean(grad * hat, axis=-1, keepdims=True)
    )


def tile(ref, s, step):
    block = ref[pl.ds(s * step, step)]
    return block.reshape(-1, block.shape[-1])


def put(ref, s, step, value):
    ref[pl.ds(s * step, step)] = value.reshape((step,) + ref.shape[1:]).astype(ref.dtype)


def first_step(axes):
    first = pl.program_id(0) == 0
    for axis in range(1, axes):
        first = jnp.logical_and(first, pl.program_id(axis) == 0)
    return first


def dx_kernel(step, chained, pair, product, go, w, norms, *rest):
    acc_in = rest[1] if chained else None
    dx, dol, acc = rest[-3:]
    c = pair.shape[-1]

    @pl.when(first_step(2))
    def _():
        acc[...] = acc_in[...] if chained else jnp.zeros_like(acc)

    def body(s, carry):
        hat, _ = layer_normalize(tile(pair, s, step).astype(F32))
        zn = (hat * norms[0:1] + norms[1:2]).astype(BF16)
        og = sigmoid(dot(zn, w[4]))
        xhat, inv2 = layer_normalize(tile(product, s, step).astype(F32))
        xn = (xhat * norms[2:3] + norms[3:4]).astype(BF16)
        y = dot(xn, w[5])
        gof = tile(go, s, step).astype(F32)
        d_y = (gof * og).astype(BF16)
        d_xn = dot_t(d_y, w[5])
        put(dx, s, step, layer_norm_backward(d_xn * norms[2:3], xhat, inv2))
        put(dol, s, step, gof * y * og * (1.0 - og))
        acc[5 * c : 6 * c] += t_dot(xn, d_y)
        acc[6 * c + 2 : 6 * c + 3] += jnp.sum(d_xn * xhat, axis=0, keepdims=True)
        acc[6 * c + 3 : 6 * c + 4] += jnp.sum(d_xn, axis=0, keepdims=True)
        return carry

    lax.fori_loop(0, pair.shape[0] // step, body, 0)


def dx_chunk(pair, product, go, weights, norms, off, size, chain):
    rows, cols, c = pair.shape
    jb = 16 if size % 16 == 0 else size
    ib = 80 if rows % 80 == 0 else rows // 2 if rows % 2 == 0 else rows
    step = 40 if ib % 40 == 0 else ib
    base = off // jb
    blk = pl.BlockSpec((ib, jb, c), lambda i, j: (i, base + j, 0))
    out = pl.BlockSpec((ib, jb, c), lambda i, j: (i, j, 0))
    full = lambda shape: pl.BlockSpec(shape, lambda i, j: (0,) * len(shape))
    n = rows * size
    acc = (6 * c + 32, c)
    return pl.pallas_call(
        functools.partial(dx_kernel, step, bool(chain)),
        grid=(rows // ib, size // jb),
        in_specs=[blk, blk, blk, full(weights.shape), full(norms.shape)]
        + ([pl.BlockSpec(memory_space=pl.ANY), full(acc)] if chain else []),
        out_specs=[out, blk, full(acc)],
        out_shape=[
            jax.ShapeDtypeStruct((rows, size, c), BF16),
            jax.ShapeDtypeStruct((rows, cols, c), BF16),
            jax.ShapeDtypeStruct(acc, F32),
        ],
        input_output_aliases={5: 1} if chain else {},
        compiler_params=pltpu.CompilerParams(vmem_limit_bytes=VMEM_LIMIT),
        cost_estimate=pl.CostEstimate(
            flops=8 * n * c * c, bytes_accessed=10 * n * c, transcendentals=n * c
        ),
        name="dx_part",
    )(pair, product, go, weights, norms, *chain)


def proj_kernel(step, pair, valid, w, norms, a, b, g_ga, g_pa, g_gb, g_pb, flip):
    cols, c = pair.shape[1:]

    def body(s, carry):
        hat, _ = layer_normalize(tile(pair, s, step).astype(F32))
        zn = (hat * norms[0:1] + norms[1:2]).astype(BF16)
        m = tile(valid, s, step).astype(F32)
        for at, d_gate, d_value in ((0, g_ga, g_pa), (2, g_gb, g_pb)):
            gate = sigmoid(dot(zn, w[at]))
            p = dot(zn, w[at + 1])
            mg = m * gate
            mgp = mg * p
            if at == 0:
                put(a, s, step, mgp)
            else:
                flip[pl.ds(s * step, step)] = mgp.reshape(step, cols, c)
            put(d_value, s, step, mg)
            put(d_gate, s, step, mgp * (1.0 - gate))
        return carry

    lax.fori_loop(0, pair.shape[0] // step, body, 0)
    b[...] = jnp.swapaxes(flip[...], 0, 1).astype(b.dtype)


def projections(pair, valid, weights, norms):
    rows, cols, c = pair.shape
    ib = 16 if rows % 16 == 0 else rows
    step = ib
    blk = pl.BlockSpec((ib, cols, c), lambda i: (i, 0, 0))
    swapped = pl.BlockSpec((cols, ib, c), lambda i: (0, i, 0))
    full = lambda shape: pl.BlockSpec(shape, lambda i: (0,) * len(shape))
    n = rows * cols
    kept = jax.ShapeDtypeStruct((rows, cols, c), BF16)
    return pl.pallas_call(
        functools.partial(proj_kernel, step),
        grid=(rows // ib,),
        in_specs=[blk, blk, full(weights.shape), full(norms.shape)],
        out_specs=[blk, swapped] + [blk] * 4,
        out_shape=[kept, jax.ShapeDtypeStruct((cols, rows, c), BF16)] + [kept] * 4,
        scratch_shapes=[pltpu.VMEM((ib, cols, c), F32)],
        compiler_params=pltpu.CompilerParams(vmem_limit_bytes=VMEM_LIMIT),
        cost_estimate=pl.CostEstimate(
            flops=8 * n * c * c, bytes_accessed=16 * n * c, transcendentals=2 * n * c
        ),
        name="projections",
    )(pair, valid, weights, norms)


def to_channels_kernel(slots, r, *refs):
    out = refs[-1]
    blocks = [ref[...].reshape(ref.shape[-3:]) for ref in refs[:-1]]
    x = jnp.concatenate(blocks, axis=1)
    out[...] = jnp.transpose(x, (2, 0, 1))


def to_channels(arrays, specs, r, lead, size, c):
    slots = len(specs)
    lanes = slots * size
    n = lead * lanes * c
    return pl.pallas_call(
        functools.partial(to_channels_kernel, slots),
        grid_spec=pltpu.PrefetchScalarGridSpec(
            num_scalar_prefetch=1,
            grid=(lead // 16,),
            in_specs=specs,
            out_specs=pl.BlockSpec((c, 16, lanes), lambda i, r: (0, i, 0)),
        ),
        out_shape=jax.ShapeDtypeStruct((c, lead, lanes), BF16),
        compiler_params=pltpu.CompilerParams(vmem_limit_bytes=VMEM_LIMIT),
        cost_estimate=pl.CostEstimate(flops=4 * n, bytes_accessed=4 * n, transcendentals=0),
        name="to_channels",
    )(r, *arrays)


def gathered_to_channels(g, r, at, size):
    n, rows, _, c = g.shape
    specs = [
        pl.BlockSpec((1, 16, size, c), lambda i, r, t=t: (r[0] ^ t, i, at, 0)) for t in range(n)
    ]
    return to_channels([g] * n, specs, r, rows, size, c)


def slots_to_channels(slots, r, off, size):
    lead, _, c = slots[0].shape
    specs = [pl.BlockSpec((16, size, c), lambda i, r: (i, off // size, 0))] * len(slots)
    return to_channels(slots, specs, r, lead, size, c)


def from_channels_kernel(slots, x, kept, sent):
    y = jnp.transpose(x[...], (1, 2, 0))
    size = y.shape[1] // slots
    for t in range(slots):
        out = sent if t % 2 else kept
        out[t // 2] = y[:, t * size : (t + 1) * size]


def from_channels(x, slots):
    c, lead, lanes = x.shape
    size = lanes // slots
    n = x.size
    out = pl.BlockSpec((slots // 2, 16, size, c), lambda i: (0, i, 0, 0))
    return pl.pallas_call(
        functools.partial(from_channels_kernel, slots),
        grid=(lead // 16,),
        in_specs=[pl.BlockSpec((c, 16, lanes), lambda i: (0, i, 0))],
        out_specs=[out, out],
        out_shape=[jax.ShapeDtypeStruct((slots // 2, lead, size, c), BF16)] * 2,
        compiler_params=pltpu.CompilerParams(vmem_limit_bytes=VMEM_LIMIT),
        cost_estimate=pl.CostEstimate(flops=4 * n, bytes_accessed=4 * n, transcendentals=0),
        name="from_channels",
    )(x)


def final_kernel(step, chained, pair, da0, da1, db0, db1, g_ga, g_pa, g_gb, g_pb, dol, wcat, norms, acc_in, *rest):
    gp, acc, flip = rest[-3:]
    c = pair.shape[-1]

    @pl.when(first_step(1))
    def _():
        acc[...] = acc_in[...]

    flip[...] = jnp.swapaxes(db0[...].astype(F32) + db1[...].astype(F32), 0, 1)

    def body(s, carry):
        hat, inv = layer_normalize(tile(pair, s, step).astype(F32))
        zn = (hat * norms[0:1] + norms[1:2]).astype(BF16)
        dav = tile(da0, s, step).astype(F32) + tile(da1, s, step).astype(F32)
        dbv = tile(flip, s, step)
        parts = [
            (dav * tile(g_ga, s, step).astype(F32)).astype(BF16),
            (dav * tile(g_pa, s, step).astype(F32)).astype(BF16),
            (dbv * tile(g_gb, s, step).astype(F32)).astype(BF16),
            (dbv * tile(g_pb, s, step).astype(F32)).astype(BF16),
            tile(dol, s, step),
        ]
        cat = jnp.concatenate(parts, axis=1)
        dzn = dot_t(cat, wcat[...])
        put(gp, s, step, layer_norm_backward(dzn * norms[0:1], hat, inv))
        grads = t_dot(zn, cat)
        for at in range(5):
            acc[at * c : (at + 1) * c] += grads[:, at * c : (at + 1) * c]
        acc[6 * c : 6 * c + 1] += jnp.sum(dzn * hat, axis=0, keepdims=True)
        acc[6 * c + 1 : 6 * c + 2] += jnp.sum(dzn, axis=0, keepdims=True)
        return carry

    lax.fori_loop(0, pair.shape[0] // step, body, 0)


def final_chunk(pair, da, db0, db1, gs, dol, wcat, norms, acc, off, size, chain):
    rows, cols, c = pair.shape
    ib = 16 if size % 16 == 0 else size
    step = ib
    base = off // ib
    blk = pl.BlockSpec((ib, cols, c), lambda i: (base + i, 0, 0))
    own = pl.BlockSpec((cols, ib, c), lambda i: (0, i, 0))
    full = lambda shape: pl.BlockSpec(shape, lambda i: (0,) * len(shape))
    n = size * cols
    return pl.pallas_call(
        functools.partial(final_kernel, step, bool(chain)),
        grid=(size // ib,),
        in_specs=[blk, blk, blk, own, own]
        + [blk] * 5
        + [full(wcat.shape), full(norms.shape), full(acc.shape)]
        + ([pl.BlockSpec(memory_space=pl.ANY)] if chain else []),
        out_specs=[blk, full(acc.shape)],
        out_shape=[
            jax.ShapeDtypeStruct((rows, cols, c), BF16),
            jax.ShapeDtypeStruct(acc.shape, F32),
        ],
        input_output_aliases={13: 0} if chain else {},
        scratch_shapes=[pltpu.VMEM((ib, cols, c), F32)],
        compiler_params=pltpu.CompilerParams(vmem_limit_bytes=VMEM_LIMIT),
        cost_estimate=pl.CostEstimate(
            flops=20 * n * c * c, bytes_accessed=22 * n * c, transcendentals=n
        ),
        name="final_part",
    )(pair, *da, db0, db1, *gs, dol, wcat, norms, acc, *chain)


def swap(v, axis, n, bit):
    return lax.ppermute(v, axis, [(r, r ^ bit) for r in range(n)])


def pick(v, at):
    return lax.dynamic_index_in_dim(v, at, 0, keepdims=False)


def bits_of(n):
    return [1 << k for k in range(n.bit_length() - 1)]


def chip_slots(v, n):
    slots = {0: v}
    for bit in bits_of(n)[:0:-1]:
        slots.update({t ^ bit: swap(x, "row", n, bit) for t, x in slots.items()})
    return [slots[t] for t in range(0, n, 2)]


def core_slots(slots, n):
    return [x for v in slots for x in (v, swap(v, "row", n, 1))]


def reduce_cores(kept, sent, n):
    come = swap(sent, "row", n, 1)
    if n == 2:
        return kept, come
    return (kept.astype(F32) + come.astype(F32)).astype(BF16), None


def reduce_chips(v, come, n):
    if come is not None:
        return v[0], come[0]
    for bit in bits_of(n)[1:]:
        v = v.reshape((-1, 2) + v.shape[1:])
        kept, come = v[:, 0], swap(v[:, 1], "row", n, bit)
        v = (kept.astype(F32) + come.astype(F32)).astype(BF16)
    return kept[0], come[0]


def tree_sum(terms):
    while len(terms) > 1:
        terms = [x + y for x, y in zip(terms[::2], terms[1::2])]
    return terms[0]


def sum_all(v, n_row, n_col):
    r = lax.axis_index("row")
    parts = v.reshape((n_row, -1) + v.shape[1:])
    terms = [pick(parts, r)]
    terms += [swap(pick(parts, r ^ t), "row", n_row, t) for t in range(1, n_row)]
    v = tree_sum(terms)
    v = tree_sum([v] + [swap(v, "col", n_col, t) for t in range(1, n_col)])
    slots = jnp.stack([v] + [swap(v, "row", n_row, t) for t in range(1, n_row)])
    return jnp.concatenate([pick(slots, r ^ p) for p in range(n_row)])


def triangles_plain(n_row, n_col, dx, a, b_swapped):
    rows, cols, c = dx.shape
    block = lax.all_gather(dx, "col", axis=1, tiled=True)
    b_all = lax.all_gather(b_swapped, "row", axis=1, tiled=True)
    part = jnp.einsum("ijc,ikc->kjc", block, a, preferred_element_type=F32).astype(BF16)
    db = lax.psum_scatter(part, "row", scatter_dimension=1, tiled=True)
    da = jnp.einsum("ijc,kjc->ikc", block, b_all, preferred_element_type=F32)
    return [da.astype(BF16)], [(db, jnp.zeros_like(db))], [(0, rows)]


def to_pairs(terms, major):
    total = terms[0]
    if len(terms) > 1:
        total = sum(term.astype(F32) for term in terms).astype(BF16)
    return jnp.transpose(with_layout_constraint(total, major), (1, 2, 0))


def triangles(n, groups, size, a, b_swapped, acc):
    r = lax.axis_index("row").astype(jnp.int32).reshape(1)
    cols = b_swapped.shape[1]
    split = 2 * size if cols > 2 * size else cols
    early = chip_slots(b_swapped[:, :split], n)
    late = chip_slots(b_swapped[:, split:], n) if split < cols else []
    a_t = jnp.transpose(a, (2, 0, 1))
    first, a_t, acc = lax.optimization_barrier((groups[0], a_t, acc))
    groups = [first] + groups[1:]
    major = Layout(major_to_minor=(0, 1, 2))
    da, b_t = None, None
    db, spans, terms, pairs = [], [], [], []
    for group in groups:
        for at in range(group.shape[2] // size):
            q = len(spans)
            off = q * size
            if q > 0:
                slots, start = (b_early, off) if off < split else (b_late, off - split)
                b_t = slots_to_channels(slots, r, start, size)
                group, da, b_t = lax.optimization_barrier((group, da, b_t))
                if pairs:
                    pairs[-1] = da
                else:
                    terms[-1] = da
            dx_t = gathered_to_channels(group, r, at, size)
            part = jnp.einsum("cik,cij->ckj", a_t, dx_t, preferred_element_type=F32).astype(BF16)
            kept, sent = from_channels(part, n)
            if q == 0:
                dx_t, kept, sent, *early = lax.optimization_barrier((dx_t, kept, sent, *early))
                b_early = core_slots(early, n)
                b_t = slots_to_channels(b_early, r, off, size)
            else:
                dx_t, kept, sent = lax.optimization_barrier((dx_t, kept, sent))
            half, come = reduce_cores(kept, sent, n)
            da = jnp.einsum("cij,ckj->cik", dx_t, b_t, preferred_element_type=F32)
            da = with_layout_constraint(da.astype(BF16), major)
            if q == 0:
                da, half, *late = lax.optimization_barrier((da, half, *late))
                b_late = core_slots(late, n)
            else:
                da, half, db[-1][1] = lax.optimization_barrier((da, half, db[-1][1]))
            db.append(list(reduce_chips(half, come, n)))
            spans.append((off, size))
            terms.append(da)
            if off + 2 * size == cols:
                da = to_pairs(terms, major)
                terms = []
                pairs.append(da)
    pairs.append(to_pairs(terms, major))
    return pairs, db, spans, acc


def shards(n_row, n_col, pair, product, mask, grad_out, weights, norms):
    rows, cols, c = pair.shape
    even = n_row == n_col and n_row & (n_row - 1) == 0 and cols % 32 == 0 and rows % 16 == 0
    size = 32 if even else cols
    widths = [size] * (cols // size)
    if len(widths) > 3:
        widths[1:3] = [2 * size]
    groups, chain, off = [], [], 0
    for width in widths:
        dx, *chain = dx_chunk(pair, product, grad_out, weights, norms, off, width, chain)
        groups.append(lax.all_gather(dx, "col", axis=0) if even else dx)
        if off == 0:
            valid = jnp.broadcast_to(mask.astype(BF16)[:, :, None], pair.shape)
            a, b_swapped, *gs = projections(pair, valid, weights, norms)
            chain[1], b_swapped = lax.optimization_barrier((chain[1], b_swapped))
        off += width
    dol, acc = chain
    if even:
        da, db, spans, acc = triangles(n_row, groups, size, a, b_swapped, acc)
    else:
        da, db, spans = triangles_plain(n_row, n_col, groups[0], a, b_swapped)
    da = da if len(da) == 2 else [da[0], jnp.zeros_like(da[0])]
    wcat = jnp.transpose(weights[:5], (1, 0, 2)).reshape(c, 5 * c)
    chain = []
    for (db0, db1), (off, size) in zip(db, spans):
        grad_pair, acc = final_chunk(
            pair, da, db0, db1, gs, dol, wcat, norms, acc, off, size, chain
        )
        chain = [grad_pair]
    acc = sum_all(acc, n_row, n_col)
    return (grad_pair, acc[: 6 * c].reshape(6, c, c), acc[6 * c : 6 * c + 4])


def solution(mesh):
    in_specs = (
        P(("groups", "row"), "col", None),
        P(("groups", "row"), "col", None),
        P(("groups", "row"), "col"),
        P(("groups", "row"), "col", None),
        P(),
        P(),
    )
    out_specs = (P(("groups", "row"), "col", None), P("groups", None, None), P("groups", None))
    body = functools.partial(shards, mesh.shape["row"], mesh.shape["col"])
    return jax.shard_map(body, mesh=mesh, in_specs=in_specs, out_specs=out_specs, check_vma=False)
```

```python
import functools

import jax
import jax.numpy as jnp
from jax import lax
from jax.experimental import pallas as pl
from jax.experimental.layout import Layout, with_layout_constraint
from jax.experimental.pallas import tpu as pltpu
from jax.sharding import PartitionSpec as P

eps = 1e-05
F32 = jnp.float32
BF16 = jnp.bfloat16
VMEM_LIMIT = 48 * 1024 * 1024


def dot(x, y):
    return jnp.dot(x, y, preferred_element_type=F32)


def sigmoid(x):
    return 0.5 * jnp.tanh(0.5 * x) + 0.5


def dot_t(x, y):
    return lax.dot_general(x, y, (((1,), (1,)), ((), ())), preferred_element_type=F32)


def t_dot(x, y):
    return lax.dot_general(x, y, (((0,), (0,)), ((), ())), preferred_element_type=F32)


def layer_normalize(v):
    mean = jnp.mean(v, axis=-1, keepdims=True)
    cent = v - mean
    inv = lax.rsqrt(jnp.mean(cent * cent, axis=-1, keepdims=True) + eps)
    return cent * inv, inv


def layer_norm_backward(grad, hat, inv):
    return inv * (
        grad
        - jnp.mean(grad, axis=-1, keepdims=True)
        - hat * jnp.mean(grad * hat, axis=-1, keepdims=True)
    )


def tile(ref, s, step):
    block = ref[pl.ds(s * step, step)]
    return block.reshape(-1, block.shape[-1])


def put(ref, s, step, value):
    ref[pl.ds(s * step, step)] = value.reshape((step,) + ref.shape[1:]).astype(ref.dtype)


def first_step(axes):
    first = pl.program_id(0) == 0
    for axis in range(1, axes):
        first = jnp.logical_and(first, pl.program_id(axis) == 0)
    return first


def dx_kernel(step, chained, pair, product, go, w, norms, *rest):
    acc_in = rest[1] if chained else None
    dx, dol, acc = rest[-3:]
    c = pair.shape[-1]

    @pl.when(first_step(2))
    def _():
        acc[...] = acc_in[...] if chained else jnp.zeros_like(acc)

    def body(s, carry):
        hat, _ = layer_normalize(tile(pair, s, step).astype(F32))
        zn = (hat * norms[0:1] + norms[1:2]).astype(BF16)
        og = sigmoid(dot(zn, w[4]))
        xhat, inv2 = layer_normalize(tile(product, s, step).astype(F32))
        xn = (xhat * norms[2:3] + norms[3:4]).astype(BF16)
        y = dot(xn, w[5])
        gof = tile(go, s, step).astype(F32)
        d_y = (gof * og).astype(BF16)
        d_xn = dot_t(d_y, w[5])
        put(dx, s, step, layer_norm_backward(d_xn * norms[2:3], xhat, inv2))
        put(dol, s, step, gof * y * og * (1.0 - og))
        acc[5 * c : 6 * c] += t_dot(xn, d_y)
        acc[6 * c + 2 : 6 * c + 3] += jnp.sum(d_xn * xhat, axis=0, keepdims=True)
        acc[6 * c + 3 : 6 * c + 4] += jnp.sum(d_xn, axis=0, keepdims=True)
        return carry

    lax.fori_loop(0, pair.shape[0] // step, body, 0)


def dx_chunk(pair, product, go, weights, norms, off, size, chain):
    rows, cols, c = pair.shape
    jb = 16 if size % 16 == 0 else size
    ib = 80 if rows % 80 == 0 else rows // 2 if rows % 2 == 0 else rows
    step = 40 if ib % 40 == 0 else ib
    base = off // jb
    blk = pl.BlockSpec((ib, jb, c), lambda i, j: (i, base + j, 0))
    out = pl.BlockSpec((ib, jb, c), lambda i, j: (i, j, 0))
    full = lambda shape: pl.BlockSpec(shape, lambda i, j: (0,) * len(shape))
    n = rows * size
    acc = (6 * c + 32, c)
    return pl.pallas_call(
        functools.partial(dx_kernel, step, bool(chain)),
        grid=(rows // ib, size // jb),
        in_specs=[blk, blk, blk, full(weights.shape), full(norms.shape)]
        + ([pl.BlockSpec(memory_space=pl.ANY), full(acc)] if chain else []),
        out_specs=[out, blk, full(acc)],
        out_shape=[
            jax.ShapeDtypeStruct((rows, size, c), BF16),
            jax.ShapeDtypeStruct((rows, cols, c), BF16),
            jax.ShapeDtypeStruct(acc, F32),
        ],
        input_output_aliases={5: 1} if chain else {},
        compiler_params=pltpu.CompilerParams(vmem_limit_bytes=VMEM_LIMIT),
        cost_estimate=pl.CostEstimate(
            flops=8 * n * c * c, bytes_accessed=10 * n * c, transcendentals=n * c
        ),
        name="dx_part",
    )(pair, product, go, weights, norms, *chain)


def proj_kernel(step, pair, valid, w, norms, a, b, g_ga, g_pa, g_gb, g_pb, flip):
    cols, c = pair.shape[1:]

    def body(s, carry):
        hat, _ = layer_normalize(tile(pair, s, step).astype(F32))
        zn = (hat * norms[0:1] + norms[1:2]).astype(BF16)
        m = tile(valid, s, step).astype(F32)
        for at, d_gate, d_value in ((0, g_ga, g_pa), (2, g_gb, g_pb)):
            gate = sigmoid(dot(zn, w[at]))
            p = dot(zn, w[at + 1])
            mg = m * gate
            mgp = mg * p
            if at == 0:
                put(a, s, step, mgp)
            else:
                flip[pl.ds(s * step, step)] = mgp.reshape(step, cols, c)
            put(d_value, s, step, mg)
            put(d_gate, s, step, mgp * (1.0 - gate))
        return carry

    lax.fori_loop(0, pair.shape[0] // step, body, 0)
    b[...] = jnp.swapaxes(flip[...], 0, 1).astype(b.dtype)


def projections(pair, valid, weights, norms):
    rows, cols, c = pair.shape
    ib = 16 if rows % 16 == 0 else rows
    step = ib
    blk = pl.BlockSpec((ib, cols, c), lambda i: (i, 0, 0))
    swapped = pl.BlockSpec((cols, ib, c), lambda i: (0, i, 0))
    full = lambda shape: pl.BlockSpec(shape, lambda i: (0,) * len(shape))
    n = rows * cols
    kept = jax.ShapeDtypeStruct((rows, cols, c), BF16)
    return pl.pallas_call(
        functools.partial(proj_kernel, step),
        grid=(rows // ib,),
        in_specs=[blk, blk, full(weights.shape), full(norms.shape)],
        out_specs=[blk, swapped] + [blk] * 4,
        out_shape=[kept, jax.ShapeDtypeStruct((cols, rows, c), BF16)] + [kept] * 4,
        scratch_shapes=[pltpu.VMEM((ib, cols, c), F32)],
        compiler_params=pltpu.CompilerParams(vmem_limit_bytes=VMEM_LIMIT),
        cost_estimate=pl.CostEstimate(
            flops=8 * n * c * c, bytes_accessed=16 * n * c, transcendentals=2 * n * c
        ),
        name="projections",
    )(pair, valid, weights, norms)


def to_channels_kernel(slots, r, *refs):
    out = refs[-1]
    blocks = [ref[...].reshape(ref.shape[-3:]) for ref in refs[:-1]]
    x = jnp.concatenate(blocks, axis=1)
    out[...] = jnp.transpose(x, (2, 0, 1))


def to_channels(arrays, specs, r, lead, size, c):
    slots = len(specs)
    lanes = slots * size
    n = lead * lanes * c
    return pl.pallas_call(
        functools.partial(to_channels_kernel, slots),
        grid_spec=pltpu.PrefetchScalarGridSpec(
            num_scalar_prefetch=1,
            grid=(lead // 16,),
            in_specs=specs,
            out_specs=pl.BlockSpec((c, 16, lanes), lambda i, r: (0, i, 0)),
        ),
        out_shape=jax.ShapeDtypeStruct((c, lead, lanes), BF16),
        compiler_params=pltpu.CompilerParams(vmem_limit_bytes=VMEM_LIMIT),
        cost_estimate=pl.CostEstimate(flops=4 * n, bytes_accessed=4 * n, transcendentals=0),
        name="to_channels",
    )(r, *arrays)


def gathered_to_channels(g, r, at, size):
    n, rows, _, c = g.shape
    specs = [
        pl.BlockSpec((1, 16, size, c), lambda i, r, t=t: (r[0] ^ t, i, at, 0)) for t in range(n)
    ]
    return to_channels([g] * n, specs, r, rows, size, c)


def slots_to_channels(slots, r, off, size):
    lead, _, c = slots[0].shape
    specs = [pl.BlockSpec((16, size, c), lambda i, r: (i, off // size, 0))] * len(slots)
    return to_channels(slots, specs, r, lead, size, c)


def from_channels_kernel(slots, x, kept, sent):
    y = jnp.transpose(x[...], (1, 2, 0))
    size = y.shape[1] // slots
    for t in range(slots):
        out = sent if t % 2 else kept
        out[t // 2] = y[:, t * size : (t + 1) * size]


def from_channels(x, slots):
    c, lead, lanes = x.shape
    size = lanes // slots
    n = x.size
    out = pl.BlockSpec((slots // 2, 16, size, c), lambda i: (0, i, 0, 0))
    return pl.pallas_call(
        functools.partial(from_channels_kernel, slots),
        grid=(lead // 16,),
        in_specs=[pl.BlockSpec((c, 16, lanes), lambda i: (0, i, 0))],
        out_specs=[out, out],
        out_shape=[jax.ShapeDtypeStruct((slots // 2, lead, size, c), BF16)] * 2,
        compiler_params=pltpu.CompilerParams(vmem_limit_bytes=VMEM_LIMIT),
        cost_estimate=pl.CostEstimate(flops=4 * n, bytes_accessed=4 * n, transcendentals=0),
        name="from_channels",
    )(x)


def final_kernel(step, chained, pair, da0, da1, db0, db1, g_ga, g_pa, g_gb, g_pb, dol, wcat, norms, acc_in, *rest):
    gp, acc, flip = rest[-3:]
    c = pair.shape[-1]

    @pl.when(first_step(1))
    def _():
        acc[...] = acc_in[...]

    flip[...] = jnp.swapaxes(db0[...].astype(F32) + db1[...].astype(F32), 0, 1)

    def body(s, carry):
        hat, inv = layer_normalize(tile(pair, s, step).astype(F32))
        zn = (hat * norms[0:1] + norms[1:2]).astype(BF16)
        dav = tile(da0, s, step).astype(F32) + tile(da1, s, step).astype(F32)
        dbv = tile(flip, s, step)
        parts = [
            (dav * tile(g_ga, s, step).astype(F32)).astype(BF16),
            (dav * tile(g_pa, s, step).astype(F32)).astype(BF16),
            (dbv * tile(g_gb, s, step).astype(F32)).astype(BF16),
            (dbv * tile(g_pb, s, step).astype(F32)).astype(BF16),
            tile(dol, s, step),
        ]
        cat = jnp.concatenate(parts, axis=1)
        dzn = dot_t(cat, wcat[...])
        put(gp, s, step, layer_norm_backward(dzn * norms[0:1], hat, inv))
        grads = t_dot(zn, cat)
        for at in range(5):
            acc[at * c : (at + 1) * c] += grads[:, at * c : (at + 1) * c]
        acc[6 * c : 6 * c + 1] += jnp.sum(dzn * hat, axis=0, keepdims=True)
        acc[6 * c + 1 : 6 * c + 2] += jnp.sum(dzn, axis=0, keepdims=True)
        return carry

    lax.fori_loop(0, pair.shape[0] // step, body, 0)


def final_chunk(pair, da, db0, db1, gs, dol, wcat, norms, acc, off, size, chain):
    rows, cols, c = pair.shape
    ib = 16 if size % 16 == 0 else size
    step = ib
    base = off // ib
    blk = pl.BlockSpec((ib, cols, c), lambda i: (base + i, 0, 0))
    own = pl.BlockSpec((cols, ib, c), lambda i: (0, i, 0))
    full = lambda shape: pl.BlockSpec(shape, lambda i: (0,) * len(shape))
    n = size * cols
    return pl.pallas_call(
        functools.partial(final_kernel, step, bool(chain)),
        grid=(size // ib,),
        in_specs=[blk, blk, blk, own, own]
        + [blk] * 5
        + [full(wcat.shape), full(norms.shape), full(acc.shape)]
        + ([pl.BlockSpec(memory_space=pl.ANY)] if chain else []),
        out_specs=[blk, full(acc.shape)],
        out_shape=[
            jax.ShapeDtypeStruct((rows, cols, c), BF16),
            jax.ShapeDtypeStruct(acc.shape, F32),
        ],
        input_output_aliases={13: 0} if chain else {},
        scratch_shapes=[pltpu.VMEM((ib, cols, c), F32)],
        compiler_params=pltpu.CompilerParams(vmem_limit_bytes=VMEM_LIMIT),
        cost_estimate=pl.CostEstimate(
            flops=20 * n * c * c, bytes_accessed=22 * n * c, transcendentals=n
        ),
        name="final_part",
    )(pair, *da, db0, db1, *gs, dol, wcat, norms, acc, *chain)


def swap(v, axis, n, bit):
    return lax.ppermute(v, axis, [(r, r ^ bit) for r in range(n)])


def pick(v, at):
    return lax.dynamic_index_in_dim(v, at, 0, keepdims=False)


def bits_of(n):
    return [1 << k for k in range(n.bit_length() - 1)]


def chip_slots(v, n):
    slots = {0: v}
    for bit in bits_of(n)[:0:-1]:
        slots.update({t ^ bit: swap(x, "row", n, bit) for t, x in slots.items()})
    return [slots[t] for t in range(0, n, 2)]


def core_slots(slots, n):
    return [x for v in slots for x in (v, swap(v, "row", n, 1))]


def reduce_cores(kept, sent, n):
    come = swap(sent, "row", n, 1)
    if n == 2:
        return kept, come
    return (kept.astype(F32) + come.astype(F32)).astype(BF16), None


def reduce_chips(v, come, n):
    if come is not None:
        return v[0], come[0]
    for bit in bits_of(n)[1:]:
        v = v.reshape((-1, 2) + v.shape[1:])
        kept, come = v[:, 0], swap(v[:, 1], "row", n, bit)
        v = (kept.astype(F32) + come.astype(F32)).astype(BF16)
    return kept[0], come[0]


def tree_sum(terms):
    while len(terms) > 1:
        terms = [x + y for x, y in zip(terms[::2], terms[1::2])]
    return terms[0]


def sum_all(v, n_row, n_col):
    r = lax.axis_index("row")
    parts = v.reshape((n_row, -1) + v.shape[1:])
    terms = [pick(parts, r)]
    terms += [swap(pick(parts, r ^ t), "row", n_row, t) for t in range(1, n_row)]
    v = tree_sum(terms)
    v = tree_sum([v] + [swap(v, "col", n_col, t) for t in range(1, n_col)])
    slots = jnp.stack([v] + [swap(v, "row", n_row, t) for t in range(1, n_row)])
    return jnp.concatenate([pick(slots, r ^ p) for p in range(n_row)])


def triangles_plain(n_row, n_col, dx, a, b_swapped):
    rows, cols, c = dx.shape
    block = lax.all_gather(dx, "col", axis=1, tiled=True)
    b_all = lax.all_gather(b_swapped, "row", axis=1, tiled=True)
    part = jnp.einsum("ijc,ikc->kjc", block, a, preferred_element_type=F32).astype(BF16)
    db = lax.psum_scatter(part, "row", scatter_dimension=1, tiled=True)
    da = jnp.einsum("ijc,kjc->ikc", block, b_all, preferred_element_type=F32)
    return [da.astype(BF16)], [(db, jnp.zeros_like(db))], [(0, rows)]


def to_pairs(terms, major):
    total = terms[0]
    if len(terms) > 1:
        total = sum(term.astype(F32) for term in terms).astype(BF16)
    return jnp.transpose(with_layout_constraint(total, major), (1, 2, 0))


def triangles(n, groups, size, a, b_swapped, acc):
    r = lax.axis_index("row").astype(jnp.int32).reshape(1)
    cols = b_swapped.shape[1]
    split = 2 * size if cols > 2 * size else cols
    early = chip_slots(b_swapped[:, :split], n)
    late = chip_slots(b_swapped[:, split:], n) if split < cols else []
    a_t = jnp.transpose(a, (2, 0, 1))
    first, a_t, acc = lax.optimization_barrier((groups[0], a_t, acc))
    groups = [first] + groups[1:]
    major = Layout(major_to_minor=(0, 1, 2))
    da, b_t = None, None
    db, spans, terms, pairs = [], [], [], []
    for group in groups:
        for at in range(group.shape[2] // size):
            q = len(spans)
            off = q * size
            if q > 0:
                slots, start = (b_early, off) if off < split else (b_late, off - split)
                b_t = slots_to_channels(slots, r, start, size)
                if pairs:
                    group, da, b_t, db[-1][1] = lax.optimization_barrier((group, da, b_t, db[-1][1]))
                    pairs[-1] = da
                else:
                    group, da, b_t = lax.optimization_barrier((group, da, b_t))
                    terms[-1] = da
            dx_t = gathered_to_channels(group, r, at, size)
            part = jnp.einsum("cik,cij->ckj", a_t, dx_t, preferred_element_type=F32).astype(BF16)
            kept, sent = from_channels(part, n)
            if q == 0:
                dx_t, kept, sent, *early = lax.optimization_barrier((dx_t, kept, sent, *early))
                b_early = core_slots(early, n)
                b_t = slots_to_channels(b_early, r, off, size)
            else:
                dx_t, kept, sent = lax.optimization_barrier((dx_t, kept, sent))
            half, come = reduce_cores(kept, sent, n)
            da = jnp.einsum("cij,ckj->cik", dx_t, b_t, preferred_element_type=F32)
            da = with_layout_constraint(da.astype(BF16), major)
            if q == 0:
                da, half, *late = lax.optimization_barrier((da, half, *late))
                b_late = core_slots(late, n)
            elif pairs:
                da, half = lax.optimization_barrier((da, half))
            else:
                da, half, db[-1][1] = lax.optimization_barrier((da, half, db[-1][1]))
            db.append(list(reduce_chips(half, come, n)))
            spans.append((off, size))
            terms.append(da)
            if off + 2 * size == cols:
                da = to_pairs(terms, major)
                terms = []
                pairs.append(da)
    pairs.append(to_pairs(terms, major))
    return pairs, db, spans, acc


def shards(n_row, n_col, pair, product, mask, grad_out, weights, norms):
    rows, cols, c = pair.shape
    even = n_row == n_col and n_row & (n_row - 1) == 0 and cols % 32 == 0 and rows % 16 == 0
    size = 32 if even else cols
    widths = [size] * (cols // size)
    groups, chain, off = [], [], 0
    for width in widths:
        dx, *chain = dx_chunk(pair, product, grad_out, weights, norms, off, width, chain)
        groups.append(lax.all_gather(dx, "col", axis=0) if even else dx)
        if off == 0:
            valid = jnp.broadcast_to(mask.astype(BF16)[:, :, None], pair.shape)
            a, b_swapped, *gs = projections(pair, valid, weights, norms)
            chain[1], b_swapped = lax.optimization_barrier((chain[1], b_swapped))
        off += width
    dol, acc = chain
    if even:
        da, db, spans, acc = triangles(n_row, groups, size, a, b_swapped, acc)
    else:
        da, db, spans = triangles_plain(n_row, n_col, groups[0], a, b_swapped)
    da = da if len(da) == 2 else [da[0], jnp.zeros_like(da[0])]
    wcat = jnp.transpose(weights[:5], (1, 0, 2)).reshape(c, 5 * c)
    chain = []
    for (db0, db1), (off, size) in zip(db, spans):
        grad_pair, acc = final_chunk(
            pair, da, db0, db1, gs, dol, wcat, norms, acc, off, size, chain
        )
        chain = [grad_pair]
    acc = sum_all(acc, n_row, n_col)
    return (grad_pair, acc[: 6 * c].reshape(6, c, c), acc[6 * c : 6 * c + 4])


def solution(mesh):
    in_specs = (
        P(("groups", "row"), "col", None),
        P(("groups", "row"), "col", None),
        P(("groups", "row"), "col"),
        P(("groups", "row"), "col", None),
        P(),
        P(),
    )
    out_specs = (P(("groups", "row"), "col", None), P("groups", None, None), P("groups", None))
    body = functools.partial(shards, mesh.shape["row"], mesh.shape["col"])
    return jax.shard_map(body, mesh=mesh, in_specs=in_specs, out_specs=out_specs, check_vma=False)
```

```python
import functools

import jax
import jax.numpy as jnp
from jax import lax
from jax.experimental import pallas as pl
from jax.experimental.layout import Layout, with_layout_constraint
from jax.experimental.pallas import tpu as pltpu
from jax.sharding import PartitionSpec as P

eps = 1e-05
F32 = jnp.float32
BF16 = jnp.bfloat16
VMEM_LIMIT = 48 * 1024 * 1024


def dot(x, y):
    return jnp.dot(x, y, preferred_element_type=F32)


def sigmoid(x):
    return 0.5 * jnp.tanh(0.5 * x) + 0.5


def dot_t(x, y):
    return lax.dot_general(x, y, (((1,), (1,)), ((), ())), preferred_element_type=F32)


def t_dot(x, y):
    return lax.dot_general(x, y, (((0,), (0,)), ((), ())), preferred_element_type=F32)


def layer_normalize(v):
    mean = jnp.mean(v, axis=-1, keepdims=True)
    cent = v - mean
    inv = lax.rsqrt(jnp.mean(cent * cent, axis=-1, keepdims=True) + eps)
    return cent * inv, inv


def layer_norm_backward(grad, hat, inv):
    return inv * (
        grad
        - jnp.mean(grad, axis=-1, keepdims=True)
        - hat * jnp.mean(grad * hat, axis=-1, keepdims=True)
    )


def tile(ref, s, step):
    block = ref[pl.ds(s * step, step)]
    return block.reshape(-1, block.shape[-1])


def put(ref, s, step, value):
    ref[pl.ds(s * step, step)] = value.reshape((step,) + ref.shape[1:]).astype(ref.dtype)


def first_step(axes):
    first = pl.program_id(0) == 0
    for axis in range(1, axes):
        first = jnp.logical_and(first, pl.program_id(axis) == 0)
    return first


def dx_kernel(step, chained, pair, product, go, w, norms, *rest):
    acc_in = rest[1] if chained else None
    dx, dol, acc = rest[-3:]
    c = pair.shape[-1]

    @pl.when(first_step(2))
    def _():
        acc[...] = acc_in[...] if chained else jnp.zeros_like(acc)

    def body(s, carry):
        hat, _ = layer_normalize(tile(pair, s, step).astype(F32))
        zn = (hat * norms[0:1] + norms[1:2]).astype(BF16)
        og = sigmoid(dot(zn, w[4]))
        xhat, inv2 = layer_normalize(tile(product, s, step).astype(F32))
        xn = (xhat * norms[2:3] + norms[3:4]).astype(BF16)
        y = dot(xn, w[5])
        gof = tile(go, s, step).astype(F32)
        d_y = (gof * og).astype(BF16)
        d_xn = dot_t(d_y, w[5])
        put(dx, s, step, layer_norm_backward(d_xn * norms[2:3], xhat, inv2))
        put(dol, s, step, gof * y * og * (1.0 - og))
        acc[5 * c : 6 * c] += t_dot(xn, d_y)
        acc[6 * c + 2 : 6 * c + 3] += jnp.sum(d_xn * xhat, axis=0, keepdims=True)
        acc[6 * c + 3 : 6 * c + 4] += jnp.sum(d_xn, axis=0, keepdims=True)
        return carry

    lax.fori_loop(0, pair.shape[0] // step, body, 0)


def dx_chunk(pair, product, go, weights, norms, off, size, chain):
    rows, cols, c = pair.shape
    jb = 16 if size % 16 == 0 else size
    ib = 80 if rows % 80 == 0 else rows // 2 if rows % 2 == 0 else rows
    step = 40 if ib % 40 == 0 else ib
    base = off // jb
    blk = pl.BlockSpec((ib, jb, c), lambda i, j: (i, base + j, 0))
    out = pl.BlockSpec((ib, jb, c), lambda i, j: (i, j, 0))
    full = lambda shape: pl.BlockSpec(shape, lambda i, j: (0,) * len(shape))
    n = rows * size
    acc = (6 * c + 32, c)
    return pl.pallas_call(
        functools.partial(dx_kernel, step, bool(chain)),
        grid=(rows // ib, size // jb),
        in_specs=[blk, blk, blk, full(weights.shape), full(norms.shape)]
        + ([pl.BlockSpec(memory_space=pl.ANY), full(acc)] if chain else []),
        out_specs=[out, blk, full(acc)],
        out_shape=[
            jax.ShapeDtypeStruct((rows, size, c), BF16),
            jax.ShapeDtypeStruct((rows, cols, c), BF16),
            jax.ShapeDtypeStruct(acc, F32),
        ],
        input_output_aliases={5: 1} if chain else {},
        compiler_params=pltpu.CompilerParams(vmem_limit_bytes=VMEM_LIMIT),
        cost_estimate=pl.CostEstimate(
            flops=8 * n * c * c, bytes_accessed=10 * n * c, transcendentals=n * c
        ),
        name="dx_part",
    )(pair, product, go, weights, norms, *chain)


def proj_kernel(step, pair, valid, w, norms, a, b, g_ga, g_pa, g_gb, g_pb, flip):
    cols, c = pair.shape[1:]

    def body(s, carry):
        hat, _ = layer_normalize(tile(pair, s, step).astype(F32))
        zn = (hat * norms[0:1] + norms[1:2]).astype(BF16)
        m = tile(valid, s, step).astype(F32)
        for at, d_gate, d_value in ((0, g_ga, g_pa), (2, g_gb, g_pb)):
            gate = sigmoid(dot(zn, w[at]))
            p = dot(zn, w[at + 1])
            mg = m * gate
            mgp = mg * p
            if at == 0:
                put(a, s, step, mgp)
            else:
                flip[pl.ds(s * step, step)] = mgp.reshape(step, cols, c)
            put(d_value, s, step, mg)
            put(d_gate, s, step, mgp * (1.0 - gate))
        return carry

    lax.fori_loop(0, pair.shape[0] // step, body, 0)
    b[...] = jnp.swapaxes(flip[...], 0, 1).astype(b.dtype)


def projections(pair, valid, weights, norms):
    rows, cols, c = pair.shape
    ib = 16 if rows % 16 == 0 else rows
    step = ib
    blk = pl.BlockSpec((ib, cols, c), lambda i: (i, 0, 0))
    swapped = pl.BlockSpec((cols, ib, c), lambda i: (0, i, 0))
    full = lambda shape: pl.BlockSpec(shape, lambda i: (0,) * len(shape))
    n = rows * cols
    kept = jax.ShapeDtypeStruct((rows, cols, c), BF16)
    return pl.pallas_call(
        functools.partial(proj_kernel, step),
        grid=(rows // ib,),
        in_specs=[blk, blk, full(weights.shape), full(norms.shape)],
        out_specs=[blk, swapped] + [blk] * 4,
        out_shape=[kept, jax.ShapeDtypeStruct((cols, rows, c), BF16)] + [kept] * 4,
        scratch_shapes=[pltpu.VMEM((ib, cols, c), F32)],
        compiler_params=pltpu.CompilerParams(vmem_limit_bytes=VMEM_LIMIT),
        cost_estimate=pl.CostEstimate(
            flops=8 * n * c * c, bytes_accessed=16 * n * c, transcendentals=2 * n * c
        ),
        name="projections",
    )(pair, valid, weights, norms)


def to_channels_kernel(slots, r, *refs):
    out = refs[-1]
    blocks = [ref[...].reshape(ref.shape[-3:]) for ref in refs[:-1]]
    x = jnp.concatenate(blocks, axis=1)
    out[...] = jnp.transpose(x, (2, 0, 1))


def to_channels(arrays, specs, r, lead, size, c):
    slots = len(specs)
    lanes = slots * size
    n = lead * lanes * c
    return pl.pallas_call(
        functools.partial(to_channels_kernel, slots),
        grid_spec=pltpu.PrefetchScalarGridSpec(
            num_scalar_prefetch=1,
            grid=(lead // 16,),
            in_specs=specs,
            out_specs=pl.BlockSpec((c, 16, lanes), lambda i, r: (0, i, 0)),
        ),
        out_shape=jax.ShapeDtypeStruct((c, lead, lanes), BF16),
        compiler_params=pltpu.CompilerParams(vmem_limit_bytes=VMEM_LIMIT),
        cost_estimate=pl.CostEstimate(flops=4 * n, bytes_accessed=4 * n, transcendentals=0),
        name="to_channels",
    )(r, *arrays)


def gathered_to_channels(g, r, at, size):
    n, rows, _, c = g.shape
    specs = [
        pl.BlockSpec((1, 16, size, c), lambda i, r, t=t: (r[0] ^ t, i, at, 0)) for t in range(n)
    ]
    return to_channels([g] * n, specs, r, rows, size, c)


def slots_to_channels(slots, r, off, size):
    lead, _, c = slots[0].shape
    specs = [pl.BlockSpec((16, size, c), lambda i, r: (i, off // size, 0))] * len(slots)
    return to_channels(slots, specs, r, lead, size, c)


def from_channels_kernel(slots, x, kept, sent):
    y = jnp.transpose(x[...], (1, 2, 0))
    size = y.shape[1] // slots
    for t in range(slots):
        out = sent if t % 2 else kept
        out[t // 2] = y[:, t * size : (t + 1) * size]


def from_channels(x, slots):
    c, lead, lanes = x.shape
    size = lanes // slots
    n = x.size
    out = pl.BlockSpec((slots // 2, 16, size, c), lambda i: (0, i, 0, 0))
    return pl.pallas_call(
        functools.partial(from_channels_kernel, slots),
        grid=(lead // 16,),
        in_specs=[pl.BlockSpec((c, 16, lanes), lambda i: (0, i, 0))],
        out_specs=[out, out],
        out_shape=[jax.ShapeDtypeStruct((slots // 2, lead, size, c), BF16)] * 2,
        compiler_params=pltpu.CompilerParams(vmem_limit_bytes=VMEM_LIMIT),
        cost_estimate=pl.CostEstimate(flops=4 * n, bytes_accessed=4 * n, transcendentals=0),
        name="from_channels",
    )(x)


def final_kernel(step, chained, pair, da0, da1, db0, db1, g_ga, g_pa, g_gb, g_pb, dol, wcat, norms, acc_in, *rest):
    gp, acc, flip = rest[-3:]
    c = pair.shape[-1]

    @pl.when(first_step(1))
    def _():
        acc[...] = acc_in[...]

    flip[...] = jnp.swapaxes(db0[...].astype(F32) + db1[...].astype(F32), 0, 1)

    def body(s, carry):
        hat, inv = layer_normalize(tile(pair, s, step).astype(F32))
        zn = (hat * norms[0:1] + norms[1:2]).astype(BF16)
        dav = tile(da0, s, step).astype(F32) + tile(da1, s, step).astype(F32)
        dbv = tile(flip, s, step)
        parts = [
            (dav * tile(g_ga, s, step).astype(F32)).astype(BF16),
            (dav * tile(g_pa, s, step).astype(F32)).astype(BF16),
            (dbv * tile(g_gb, s, step).astype(F32)).astype(BF16),
            (dbv * tile(g_pb, s, step).astype(F32)).astype(BF16),
            tile(dol, s, step),
        ]
        cat = jnp.concatenate(parts, axis=1)
        dzn = dot_t(cat, wcat[...])
        put(gp, s, step, layer_norm_backward(dzn * norms[0:1], hat, inv))
        grads = t_dot(zn, cat)
        for at in range(5):
            acc[at * c : (at + 1) * c] += grads[:, at * c : (at + 1) * c]
        acc[6 * c : 6 * c + 1] += jnp.sum(dzn * hat, axis=0, keepdims=True)
        acc[6 * c + 1 : 6 * c + 2] += jnp.sum(dzn, axis=0, keepdims=True)
        return carry

    lax.fori_loop(0, pair.shape[0] // step, body, 0)


def final_chunk(pair, da, db0, db1, gs, dol, wcat, norms, acc, off, size, chain):
    rows, cols, c = pair.shape
    ib = 16 if size % 16 == 0 else size
    step = ib
    base = off // ib
    blk = pl.BlockSpec((ib, cols, c), lambda i: (base + i, 0, 0))
    own = pl.BlockSpec((cols, ib, c), lambda i: (0, i, 0))
    full = lambda shape: pl.BlockSpec(shape, lambda i: (0,) * len(shape))
    n = size * cols
    return pl.pallas_call(
        functools.partial(final_kernel, step, bool(chain)),
        grid=(size // ib,),
        in_specs=[blk, blk, blk, own, own]
        + [blk] * 5
        + [full(wcat.shape), full(norms.shape), full(acc.shape)]
        + ([pl.BlockSpec(memory_space=pl.ANY)] if chain else []),
        out_specs=[blk, full(acc.shape)],
        out_shape=[
            jax.ShapeDtypeStruct((rows, cols, c), BF16),
            jax.ShapeDtypeStruct(acc.shape, F32),
        ],
        input_output_aliases={13: 0} if chain else {},
        scratch_shapes=[pltpu.VMEM((ib, cols, c), F32)],
        compiler_params=pltpu.CompilerParams(vmem_limit_bytes=VMEM_LIMIT),
        cost_estimate=pl.CostEstimate(
            flops=20 * n * c * c, bytes_accessed=22 * n * c, transcendentals=n
        ),
        name="final_part",
    )(pair, *da, db0, db1, *gs, dol, wcat, norms, acc, *chain)


def swap(v, axis, n, bit):
    return lax.ppermute(v, axis, [(r, r ^ bit) for r in range(n)])


def pick(v, at):
    return lax.dynamic_index_in_dim(v, at, 0, keepdims=False)


def bits_of(n):
    return [1 << k for k in range(n.bit_length() - 1)]


def chip_slots(v, n):
    slots = {0: v}
    for bit in bits_of(n)[:0:-1]:
        slots.update({t ^ bit: swap(x, "row", n, bit) for t, x in slots.items()})
    return [slots[t] for t in range(0, n, 2)]


def core_slots(slots, n):
    return [x for v in slots for x in (v, swap(v, "row", n, 1))]


def reduce_cores(kept, sent, n):
    come = swap(sent, "row", n, 1)
    if n == 2:
        return kept, come
    return (kept.astype(F32) + come.astype(F32)).astype(BF16), None


def reduce_chips(v, come, n):
    if come is not None:
        return v[0], come[0]
    for bit in bits_of(n)[1:]:
        v = v.reshape((-1, 2) + v.shape[1:])
        kept, come = v[:, 0], swap(v[:, 1], "row", n, bit)
        v = (kept.astype(F32) + come.astype(F32)).astype(BF16)
    return kept[0], come[0]


def tree_sum(terms):
    while len(terms) > 1:
        terms = [x + y for x, y in zip(terms[::2], terms[1::2])]
    return terms[0]


def sum_all(v, n_row, n_col):
    r = lax.axis_index("row")
    parts = v.reshape((n_row, -1) + v.shape[1:])
    terms = [pick(parts, r)]
    terms += [swap(pick(parts, r ^ t), "row", n_row, t) for t in range(1, n_row)]
    v = tree_sum(terms)
    v = tree_sum([v] + [swap(v, "col", n_col, t) for t in range(1, n_col)])
    slots = jnp.stack([v] + [swap(v, "row", n_row, t) for t in range(1, n_row)])
    return jnp.concatenate([pick(slots, r ^ p) for p in range(n_row)])


def triangles_plain(n_row, n_col, dx, a, b_swapped):
    rows, cols, c = dx.shape
    block = lax.all_gather(dx, "col", axis=1, tiled=True)
    b_all = lax.all_gather(b_swapped, "row", axis=1, tiled=True)
    part = jnp.einsum("ijc,ikc->kjc", block, a, preferred_element_type=F32).astype(BF16)
    db = lax.psum_scatter(part, "row", scatter_dimension=1, tiled=True)
    da = jnp.einsum("ijc,kjc->ikc", block, b_all, preferred_element_type=F32)
    return [da.astype(BF16)], [(db, jnp.zeros_like(db))], [(0, rows)]


def to_pairs(terms, major):
    total = terms[0]
    if len(terms) > 1:
        total = sum(term.astype(F32) for term in terms).astype(BF16)
    return jnp.transpose(with_layout_constraint(total, major), (1, 2, 0))


def triangles(n, groups, split, a, b_swapped, acc):
    r = lax.axis_index("row").astype(jnp.int32).reshape(1)
    cols = b_swapped.shape[1]
    early = chip_slots(b_swapped[:, :split], n)
    late = chip_slots(b_swapped[:, split:], n) if split < cols else []
    a_t = jnp.transpose(a, (2, 0, 1))
    first, a_t, acc = lax.optimization_barrier((groups[0], a_t, acc))
    groups = [first] + groups[1:]
    major = Layout(major_to_minor=(0, 1, 2))
    da, b_t = None, None
    db, spans, terms, pairs = [], [], [], []
    off = 0
    for q, group in enumerate(groups):
        size = group.shape[2]
        if q > 0:
            slots, start = (b_early, off) if off < split else (b_late, off - split)
            b_t = slots_to_channels(slots, r, start, size)
            if pairs:
                group, da, b_t, db[-1][1] = lax.optimization_barrier((group, da, b_t, db[-1][1]))
                pairs[-1] = da
            else:
                group, da, b_t = lax.optimization_barrier((group, da, b_t))
                terms[-1] = da
        dx_t = gathered_to_channels(group, r, 0, size)
        part = jnp.einsum("cik,cij->ckj", a_t, dx_t, preferred_element_type=F32).astype(BF16)
        kept, sent = from_channels(part, n)
        if q == 0:
            dx_t, kept, sent, *early = lax.optimization_barrier((dx_t, kept, sent, *early))
            b_early = core_slots(early, n)
            b_t = slots_to_channels(b_early, r, off, size)
        else:
            dx_t, kept, sent = lax.optimization_barrier((dx_t, kept, sent))
        half, come = reduce_cores(kept, sent, n)
        da = jnp.einsum("cij,ckj->cik", dx_t, b_t, preferred_element_type=F32)
        da = with_layout_constraint(da.astype(BF16), major)
        if q == 0:
            da, half, *late = lax.optimization_barrier((da, half, *late))
            b_late = core_slots(late, n)
        elif pairs:
            da, half = lax.optimization_barrier((da, half))
        else:
            da, half, db[-1][1] = lax.optimization_barrier((da, half, db[-1][1]))
        db.append(list(reduce_chips(half, come, n)))
        spans.append((off, size))
        terms.append(da)
        off += size
        if q == len(groups) - 2:
            da = to_pairs(terms, major)
            terms = []
            pairs.append(da)
    pairs.append(to_pairs(terms, major))
    return pairs, db, spans, acc


def shards(n_row, n_col, pair, product, mask, grad_out, weights, norms):
    rows, cols, c = pair.shape
    even = n_row == n_col and n_row & (n_row - 1) == 0 and cols % 32 == 0 and rows % 16 == 0
    if not even:
        widths, split = [cols], cols
    elif cols % 160 == 0:
        widths, split = [3 * cols // 10] * 2 + [cols // 5] * 2, 3 * cols // 5
    else:
        widths, split = [32] * (cols // 32), min(64, cols)
    groups, chain, off = [], [], 0
    for width in widths:
        dx, *chain = dx_chunk(pair, product, grad_out, weights, norms, off, width, chain)
        groups.append(lax.all_gather(dx, "col", axis=0) if even else dx)
        if off == 0:
            valid = jnp.broadcast_to(mask.astype(BF16)[:, :, None], pair.shape)
            a, b_swapped, *gs = projections(pair, valid, weights, norms)
            chain[1], b_swapped = lax.optimization_barrier((chain[1], b_swapped))
        off += width
    dol, acc = chain
    if even:
        da, db, spans, acc = triangles(n_row, groups, split, a, b_swapped, acc)
    else:
        da, db, spans = triangles_plain(n_row, n_col, groups[0], a, b_swapped)
    da = da if len(da) == 2 else [da[0], jnp.zeros_like(da[0])]
    wcat = jnp.transpose(weights[:5], (1, 0, 2)).reshape(c, 5 * c)
    chain = []
    for (db0, db1), (off, size) in zip(db, spans):
        grad_pair, acc = final_chunk(
            pair, da, db0, db1, gs, dol, wcat, norms, acc, off, size, chain
        )
        chain = [grad_pair]
    acc = sum_all(acc, n_row, n_col)
    return (grad_pair, acc[: 6 * c].reshape(6, c, c), acc[6 * c : 6 * c + 4])


def solution(mesh):
    in_specs = (
        P(("groups", "row"), "col", None),
        P(("groups", "row"), "col", None),
        P(("groups", "row"), "col"),
        P(("groups", "row"), "col", None),
        P(),
        P(),
    )
    out_specs = (P(("groups", "row"), "col", None), P("groups", None, None), P("groups", None))
    body = functools.partial(shards, mesh.shape["row"], mesh.shape["col"])
    return jax.shard_map(body, mesh=mesh, in_specs=in_specs, out_specs=out_specs, check_vma=False)
```
